32 devices in a mesh: dp: 8 (over z, core), seq: 4 (over y, x).
Axes of the slice: x: 2, y: 2, z: 4, core: 2. Of those that a mesh axis runs over, the one named last changes fastest.
Arguments:
- query_in: bfloat16 [8, 512, 2048], P('dp', 'seq'), may hold values from -6 to 6
- key_in: bfloat16 [8, 512, 2048], P('dp', 'seq'), may hold values from -6 to 6
- value_in: bfloat16 [8, 512, 2048], P('dp', 'seq'), may hold values from -6 to 6
- grad_out: bfloat16 [8, 512, 2048], P('dp', 'seq'), may hold values from -6 to 6
- w_query: bfloat16 [2048, 128], replicated, may hold values from -0.5 to 0.5
- w_key: bfloat16 [2048, 128], replicated, may hold values from -0.5 to 0.5
- norm_gain: float32 [2048], replicated, may hold values from 0.1 to 1.9
Outputs:
- grad_query: bfloat16 [8, 512, 2048], P('dp', 'seq')
- grad_key: bfloat16 [8, 512, 2048], P('dp', 'seq')
- grad_value: bfloat16 [8, 512, 2048], P('dp', 'seq')
- grad_w_query: float32 [2048, 128], P('dp')
- grad_w_key: float32 [2048, 128], P('dp')
- grad_gain: float32 [2048], P('dp')
The draws below stay inside these ranges and needn't reach their ends.
All inputs are finite; a program needn't handle non-finite values.
Results may differ from the reference program's by a relative error of at most 0.0077.
Values sent between devices are 32-bit elements; how exact they have to be, the bound alone decides.
No kernel may reach another device: no remote copies, remote signals or barrier semaphores. Data moves between devices by JAX's collectives and lax.ppermute only.
A program may use at most 128 MiB of HBM per device.

```python
import jax
import jax.numpy as jnp
from jax import lax

HEAD = 128
TOK_DEV = 128
HD = 2048
LEN = 512
BATCH = 8


def raised(values, own_key, source, target, shards_of, factor):
    def block_of(position):
        return (jnp.arange(values.shape[position]) // (values.shape[position] // shards_of)).reshape((-1,) + (1,) * (values.ndim - 1 - position))

    first = jax.random.permutation(own_key, shards_of)[block_of(target)]
    far = (block_of(target) + shards_of // 2) % shards_of
    return jnp.where((block_of(source) == first) | (block_of(source) == far), factor * values, values)


def steps_of(rng, dims, cuts, low, top_value):
    def one(position, parts):
        draws = jax.random.uniform(jax.random.fold_in(jax.random.fold_in(rng, 6), position), (parts,), jnp.float32, low / len(cuts), top_value / len(cuts))
        return jnp.repeat(jnp.exp(draws), dims[position] // parts).reshape((-1,) + (1,) * (len(dims) - position - 1))

    gain = one(*cuts[0])
    for cut in cuts[1:]:
        gain = gain * one(*cut)
    return gain


def normal_values(key, extent, deviation, limit, split=(), kind=jnp.bfloat16):
    drawn = deviation * jax.random.normal(key, extent, jnp.float32)
    if split:
        drawn = drawn * steps_of(key, extent, split, -0.22, 0.18)
    return jnp.clip(drawn, -limit, limit).astype(kind)


def bell_draw_with(stream_key, shape, scale, limit, split, heavy, kind=jnp.bfloat16):
    array = scale * jax.random.normal(stream_key, shape, jnp.float32)
    if split:
        array = array * steps_of(stream_key, shape, split, -0.22, 0.18)
    return jnp.clip(raised(array, jax.random.fold_in(stream_key, 3), *heavy), -limit, limit).astype(kind)


def setup_inputs(seed: int = 0) -> dict:
    streams_of = jax.random.split(jax.random.key(seed), 8)
    return {
        "query_in": bell_draw_with(streams_of[0], (BATCH, LEN, HD), 1.0, 6.0, ((0, 8), (1, 4)), (0, 2, 8, 2.0)),
        "key_in": bell_draw_with(streams_of[1], (BATCH, LEN, HD), 1.0, 6.0, ((0, 8), (1, 4)), (0, 2, 8, 2.0)),
        "value_in": normal_values(streams_of[2], (BATCH, LEN, HD), 1.0, 6.0, ((0, 8), (1, 4))),
        "grad_out": bell_draw_with(streams_of[3], (BATCH, LEN, HD), 1.0, 6.0, ((0, 8), (1, 4)), (0, 2, 8, 2.0)),
        "w_query": normal_values(streams_of[4], (HD, HEAD), HEAD ** -0.5, 0.5),
        "w_key": normal_values(streams_of[5], (HD, HEAD), HEAD ** -0.5, 0.5),
        "norm_gain": jnp.clip(1.0 + 0.18 * jax.random.normal(streams_of[6], (HD,), jnp.float32), 0.1, 1.9),
    }


norm_eps = 1e-05
highest = lax.Precision.HIGHEST

def rounded(tensor):
    return lax.optimization_barrier(tensor.astype(jnp.bfloat16)).astype(jnp.float32)

def one_sequence(query_in, key_in, value_in, grad_out, w_query, w_key, norm_gain):
    length, width_all = query_in.shape
    blocks = length // TOK_DEV
    head_count = width_all // HEAD

    def split_heads(tensor):
        return tensor.reshape(blocks, TOK_DEV, head_count, HEAD).astype(jnp.float32)
    query_h = split_heads(query_in)
    key_h = split_heads(key_in)
    value_h = split_heads(value_in)
    grad_f = split_heads(grad_out)
    map_query = w_query.reshape(head_count, HEAD, HEAD).astype(jnp.float32)
    map_key = w_key.reshape(head_count, HEAD, HEAD).astype(jnp.float32)
    pre_query = jnp.einsum('nthd,hde->nthe', query_h, map_query, precision=highest)
    pre_key = jnp.einsum('nthd,hde->nthe', key_h, map_key, precision=highest)
    feat_query = rounded(jax.nn.elu(pre_query) + 1.0)
    feat_key = rounded(jax.nn.elu(pre_key) + 1.0)
    causal = jnp.tril(jnp.ones((TOK_DEV, TOK_DEV), dtype=bool))
    local_state = jnp.einsum('nthf,nthe->nhfe', feat_key, value_h, precision=highest)
    zero_state = jnp.zeros((1,) + local_state.shape[1:], jnp.float32)
    prior_state = jnp.concatenate([zero_state, jnp.cumsum(local_state, axis=0)[:-1]], axis=0)
    scores = jnp.einsum('nthf,nshf->nhts', feat_query, feat_key, precision=highest)
    attn_weights = rounded(jnp.where(causal, scores, 0.0))
    numerator = jnp.einsum('nhts,nshe->nthe', attn_weights, value_h, precision=highest)
    numerator = numerator + jnp.einsum('nthf,nhfe->nthe', feat_query, prior_state, precision=highest)
    inv_rms = lax.rsqrt(lax.optimization_barrier(jnp.mean(numerator * numerator, axis=-1, keepdims=True)) + norm_eps)
    normed = numerator * inv_rms
    gain_h = norm_gain.reshape(head_count, HEAD).astype(jnp.float32)
    grad_normed = grad_f * gain_h
    grad_numer = inv_rms * (grad_normed - normed * lax.optimization_barrier(jnp.mean(grad_normed * normed, axis=-1, keepdims=True)))
    grad_gain = lax.optimization_barrier(jnp.sum(normed * grad_f, axis=(0, 1))).reshape(width_all)
    numer_low = rounded(grad_numer)
    local_adjoint = jnp.einsum('nthf,nthe->nhfe', feat_query, numer_low, precision=highest)
    reverse_sum = jnp.cumsum(local_adjoint[::-1], axis=0)[::-1]
    later_state = jnp.concatenate([reverse_sum[1:], zero_state], axis=0)
    mixed = jnp.einsum('nthe,nshe->nhts', numer_low, value_h, precision=highest)
    mixed_low = rounded(jnp.where(causal, mixed, 0.0))
    grad_fq = jnp.einsum('nhts,nshf->nthf', mixed_low, feat_key, precision=highest)
    grad_fq = grad_fq + jnp.einsum('nthe,nhfe->nthf', grad_numer, prior_state, precision=highest)
    grad_fk = jnp.einsum('nhts,nthf->nshf', mixed_low, feat_query, precision=highest)
    grad_fk = grad_fk + jnp.einsum('nshe,nhfe->nshf', value_h, later_state, precision=highest)
    grad_v = jnp.einsum('nhts,nthe->nshe', attn_weights, numer_low, precision=highest)
    grad_v = grad_v + jnp.einsum('nshf,nhfe->nshe', feat_key, later_state, precision=highest)
    pre_grad_q = rounded(grad_fq * jnp.minimum(jnp.exp(pre_query), 1.0))
    pre_grad_k = rounded(grad_fk * jnp.minimum(jnp.exp(pre_key), 1.0))
    grad_query = jnp.einsum('nthe,hde->nthd', pre_grad_q, map_query, precision=highest)
    grad_key = jnp.einsum('nthe,hde->nthd', pre_grad_k, map_key, precision=highest)
    sum_wq = jnp.einsum('nthd,nthe->hde', query_h, pre_grad_q, precision=highest).reshape(width_all, HEAD)
    sum_wk = jnp.einsum('nthd,nthe->hde', key_h, pre_grad_k, precision=highest).reshape(width_all, HEAD)
    return (grad_query.reshape(length, width_all).astype(jnp.bfloat16), grad_key.reshape(length, width_all).astype(jnp.bfloat16), grad_v.reshape(length, width_all).astype(jnp.bfloat16), sum_wq, sum_wk, grad_gain)

def reference(query_in, key_in, value_in, grad_out, w_query, w_key, norm_gain):

    def per_sequence(items):
        return one_sequence(items[0], items[1], items[2], items[3], w_query, w_key, norm_gain)
    grad_query, grad_key, grad_value, sum_wq, sum_wk, sum_gain = lax.map(per_sequence, (query_in, key_in, value_in, grad_out))
    return (grad_query, grad_key, grad_value, lax.optimization_barrier(jnp.sum(sum_wq, axis=0)), lax.optimization_barrier(jnp.sum(sum_wk, axis=0)), lax.optimization_barrier(jnp.sum(sum_gain, axis=0)))
```

```python
import functools

import jax
import jax.numpy as jnp
from jax import lax
from jax.experimental import pallas as pl
from jax.experimental.pallas import tpu as pltpu
from jax.sharding import PartitionSpec as P

HEAD = 128
GROUP = 4
NORM_EPS = 1e-05
F32 = jnp.float32
BF16 = jnp.bfloat16


def dot(a, b, ca=1, cb=0):
    return lax.dot_general(a, b, (((ca,), (cb,)), ((), ())), preferred_element_type=F32)


def feature(pre):
    return jnp.where(pre > 0.0, pre + 1.0, jnp.exp(jnp.minimum(pre, 0.0)))


def split_low(value):
    high = value.astype(BF16)
    return high, (value - high.astype(F32)).astype(BF16)


def tril(rows):
    return lax.broadcasted_iota(jnp.int32, (rows, rows), 0) >= lax.broadcasted_iota(
        jnp.int32, (rows, rows), 1
    )


def columns(offset, i):
    at = (2 * i + offset) * HEAD
    return slice(at, at + HEAD)


def key_kernel(offset, key, value, w_key, feat_key, slope, state):
    for i in range(GROUP):
        at = columns(offset, i)
        feat = feature(dot(key[:, at], w_key[at, :]))
        low = feat.astype(BF16)
        feat_key[i] = low
        slope[i] = jnp.minimum(feat, 1.0)
        state[i] = dot(low, value[:, at], 0, 0)


def query_kernel(offset, query, value, w_query, feat_key, feat_query, slope, attn, inner):
    causal = tril(query.shape[0])
    for i in range(GROUP):
        at = columns(offset, i)
        feat = feature(dot(query[:, at], w_query[at, :]))
        low = feat.astype(BF16)
        feat_query[i] = low
        slope[i] = jnp.minimum(feat, 1.0)
        weights = jnp.where(causal, dot(low, feat_key[i], 1, 1), 0.0).astype(BF16)
        attn[i] = weights
        inner[i] = dot(weights, value[:, at])


def numer_kernel(offset, keep, first, second, feat_query, inner, grad, gain, adjoint, low_out, rest_out, ph_out, pl_out, gain_out):
    keep_first = keep[0] > 0
    keep_second = keep[1] > 0
    for i in range(GROUP):
        at = columns(offset, i)
        prior = jnp.where(keep_first, first[i], 0.0) + jnp.where(keep_second, second[i], 0.0)
        high, low = split_low(prior)
        ph_out[i] = high
        pl_out[i] = low
        feat = feat_query[i]
        numer = inner[i] + dot(feat, high) + dot(feat, low)
        inv = lax.rsqrt(jnp.mean(numer * numer, axis=-1, keepdims=True) + NORM_EPS)
        normed = numer * inv
        grad_f = grad[:, at].astype(F32)
        scaled = grad_f * gain[:, at]
        grad_numer = inv * (scaled - normed * jnp.mean(scaled * normed, axis=-1, keepdims=True))
        gain_out[i] = jnp.broadcast_to(jnp.sum(normed * grad_f, axis=0, keepdims=True), (8, HEAD))
        numer_low, rest = split_low(grad_numer)
        low_out[i] = numer_low
        rest_out[i] = rest
        adjoint[i] = dot(feat, numer_low, 0, 0)


def query_grad_kernel(offset, numer_low, rest, high, low, feat_key, slope, query, value, gain, mixed_out, pre_out, weight):
    causal = tril(query.shape[0])
    rows = HEAD
    for i in range(GROUP):
        at = columns(offset, i)
        grad_low = numer_low[i]
        mixed = jnp.where(causal, dot(grad_low, value[:, at], 1, 1), 0.0).astype(BF16)
        mixed_out[i] = mixed
        grad_fq = (
            dot(mixed, feat_key[i])
            + dot(grad_low, high[i], 1, 1)
            + dot(grad_low, low[i], 1, 1)
            + dot(rest[i], high[i], 1, 1)
        )
        pre = (grad_fq * slope[i]).astype(BF16)
        pre_out[i] = pre
        weight[i, :rows, :] = dot(query[:, at], pre, 0, 0)
        weight[i, rows:, :] = gain[i]


def key_grad_kernel(offset, keep, first, second, mixed, feat_query, slope, key, value, pre_out, lh_out, ll_out, weight):
    keep_first = keep[2] > 0
    keep_second = keep[3] > 0
    for i in range(GROUP):
        at = columns(offset, i)
        later = jnp.where(keep_first, first[i], 0.0) + jnp.where(keep_second, second[i], 0.0)
        high, low = split_low(later)
        lh_out[i] = high
        ll_out[i] = low
        val = value[:, at]
        grad_fk = dot(mixed[i], feat_query[i], 0, 0) + dot(val, high, 1, 1) + dot(val, low, 1, 1)
        pre = (grad_fk * slope[i]).astype(BF16)
        pre_out[i] = pre
        weight[i] = dot(key[:, at], pre, 0, 0)


def back_kernel(groups, *refs):
    pre, w, out = refs[:groups], refs[groups], refs[groups + 1]
    for g in range(groups):
        for i in range(GROUP):
            at = place(g, i, groups)
            out[:, at] = dot(pre[g][i], w[at, :], 1, 1).astype(BF16)


def value_grad_kernel(groups, *refs):
    attn, numer_low, feat_key, high, low = (refs[k * groups : (k + 1) * groups] for k in range(5))
    out = refs[5 * groups]
    for g in range(groups):
        for i in range(GROUP):
            feat = feat_key[g][i]
            grad = dot(attn[g][i], numer_low[g][i], 0, 0) + dot(feat, high[g][i]) + dot(feat, low[g][i])
            out[:, place(g, i, groups)] = grad.astype(BF16)


def head_of(g, i, groups):
    half = groups // 2
    return (g % half) * 2 * GROUP + 2 * i + g // half


def place(g, i, groups):
    at = head_of(g, i, groups) * HEAD
    return slice(at, at + HEAD)


def call(body, ins, outs, name, flops):
    bytes_all = sum(x.size * x.dtype.itemsize for x, _ in ins if x.dtype != jnp.int32)
    return pl.pallas_call(
        body,
        grid=(1,),
        in_specs=[spec for _, spec in ins],
        out_specs=[pl.BlockSpec(shape, lambda _, n=len(shape): (0,) * n) for shape, _ in outs],
        out_shape=[jax.ShapeDtypeStruct(shape, kind) for shape, kind in outs],
        compiler_params=pltpu.CompilerParams(vmem_limit_bytes=48 * 1024 * 1024),
        cost_estimate=pl.CostEstimate(flops=flops, bytes_accessed=bytes_all, transcendentals=0),
        name=name,
    )(*[x for x, _ in ins])


def whole(x):
    return (x, pl.BlockSpec(x.shape, lambda _, n=x.ndim: (0,) * n))


def scan_generic(value, reverse):
    peers, mine = lax.axis_size("seq"), lax.axis_index("seq")
    everything = lax.all_gather(value, "seq")

    def turn(k, before):
        reached = k > mine if reverse else k < mine
        return before + jnp.where(reached, everything[k], 0.0)

    return lax.fori_loop(0, peers, turn, jnp.zeros_like(value))


def swap(value, axis, bit):
    return lax.ppermute(value, axis, [(i, i ^ bit) for i in range(lax.axis_size(axis))])


def pick(value, axis, index):
    first = index == 0
    return jnp.where(first, value[0], value[1]), jnp.where(first, value[1], value[0])


def owned_sum(weights):
    dp = lax.axis_index("dp")
    core, near, far = dp % 2, (dp // 2) % 2, dp // 4
    rows = weights.shape[1]
    by = weights.reshape(4, 2, rows, HEAD)
    kept, sent = pick(by.transpose(1, 0, 2, 3), 0, core)
    part = kept + swap(sent, "dp", 1)
    kept, sent = pick(part.reshape(2, 2, rows, HEAD).transpose(1, 0, 2, 3), 0, near)
    part = kept + swap(sent, "dp", 2)
    kept, sent = pick(part, 0, far)
    return kept + swap(sent, "dp", 4)


def square_sum(value):
    value = value + swap(value, "seq", 1)
    return value + swap(value, "seq", 2)


def per_device(query_in, key_in, value_in, grad_out, w_query, w_key, norm_gain):
    _, rows, width = query_in.shape
    heads = width // HEAD
    groups = heads // GROUP
    half = groups // 2
    tuned = lax.axis_size("seq") == 4 and lax.axis_size("dp") == 8 and heads == 16
    query, key, value, grad = (x.reshape(rows, width) for x in (query_in, key_in, value_in, grad_out))
    gain = norm_gain.reshape(1, width)
    wide = 2 * GROUP * HEAD

    def cols(x, g):
        return (x, pl.BlockSpec((x.shape[0], wide), lambda _: (0, g % half)))

    def wrows(x, g):
        return (x, pl.BlockSpec((wide, HEAD), lambda _: (g % half, 0)))

    mine = lax.axis_index("seq")
    at_x, at_y = mine % 2, mine // 2
    if tuned:
        keep = jnp.stack([at_x, at_y, 1 - at_x, 1 - at_y]).astype(jnp.int32)
    else:
        keep = jnp.array([1, 0, 1, 0], jnp.int32)
    flags = (keep, pl.BlockSpec(memory_space=pltpu.SMEM))

    def tok(kind):
        return ((GROUP, rows, HEAD), kind)

    def sq(kind):
        return ((GROUP, HEAD, HEAD), kind)

    unit = 2 * rows * HEAD * HEAD * GROUP

    def around(states, reverse):
        if not tuned:
            total = scan_generic(states, reverse)
            return total, total
        first = swap(states, "seq", 1)
        return first, swap(states + first, "seq", 2)

    feat_k, slope_k, state = [], [], []
    for g in range(groups):
        f, s, m = call(
            functools.partial(key_kernel, g // half),
            [cols(key, g), cols(value, g), wrows(w_key, g)],
            [tok(BF16), tok(F32), sq(F32)],
            f"key_state_{g}",
            2 * unit,
        )
        feat_k.append(f)
        slope_k.append(s)
        state.append(m)
    prior = [around(m, False) for m in state]
    feat_q, slope_q, attn, inner = [], [], [], []
    for g in range(groups):
        f, s, a, n = call(
            functools.partial(query_kernel, g // half),
            [cols(query, g), cols(value, g), wrows(w_query, g), whole(feat_k[g])],
            [tok(BF16), tok(F32), ((GROUP, rows, rows), BF16), tok(F32)],
            f"query_attn_{g}",
            3 * unit,
        )
        feat_q.append(f)
        slope_q.append(s)
        attn.append(a)
        inner.append(n)
    numer = []
    later = []
    for g in range(groups):
        out = call(
            functools.partial(numer_kernel, g // half),
            [flags, whole(prior[g][0]), whole(prior[g][1]), whole(feat_q[g]), whole(inner[g]), cols(grad, g), cols(gain, g)],
            [sq(F32), tok(BF16), tok(BF16), sq(BF16), sq(BF16), ((GROUP, 8, HEAD), F32)],
            f"numer_{g}",
            3 * unit,
        )
        numer.append(out)
        later.append(around(out[0], True))
    mixed, pre_q, sum_q = [], [], []
    for g in range(groups):
        _, low, rest, ph, pl_, gains = numer[g]
        m, p, w = call(
            functools.partial(query_grad_kernel, g // half),
            [whole(x) for x in (low, rest, ph, pl_, feat_k[g], slope_q[g])] + [cols(query, g), cols(value, g), whole(gains)],
            [((GROUP, rows, rows), BF16), tok(BF16), ((GROUP, HEAD + 8, HEAD), F32)],
            f"query_grad_{g}",
            6 * unit,
        )
        mixed.append(m)
        pre_q.append(p)
        sum_q.append(w)
    pre_k, late_h, late_l, sum_k = [], [], [], []
    for g in range(groups):
        p, h, l, w = call(
            functools.partial(key_grad_kernel, g // half),
            [flags, whole(later[g][0]), whole(later[g][1]), whole(mixed[g]), whole(feat_q[g]), whole(slope_k[g]), cols(key, g), cols(value, g)],
            [tok(BF16), sq(BF16), sq(BF16), sq(F32)],
            f"key_grad_{g}",
            4 * unit,
        )
        pre_k.append(p)
        late_h.append(h)
        late_l.append(l)
        sum_k.append(w)

    full = [((rows, width), BF16)]
    (grad_query,) = call(
        functools.partial(back_kernel, groups), [whole(x) for x in pre_q] + [whole(w_query)], full, "grad_query", groups * unit
    )
    (grad_key,) = call(
        functools.partial(back_kernel, groups), [whole(x) for x in pre_k] + [whole(w_key)], full, "grad_key", groups * unit
    )
    (grad_value,) = call(
        functools.partial(value_grad_kernel, groups),
        [whole(x) for x in attn + [n[1] for n in numer] + feat_k + late_h + late_l],
        full,
        "grad_value",
        3 * groups * unit,
    )

    if tuned:
        halves = [jnp.concatenate(sum_q[b * half : (b + 1) * half], axis=0) for b in range(2)]
        part_q = owned_sum(jnp.concatenate(halves, axis=1))
        part_k = [
            owned_sum(jnp.concatenate(sum_k[b * half : (b + 1) * half], axis=0)) for b in range(2)
        ]
        early = square_sum(jnp.concatenate([part_q, part_k[0]], axis=0))
        last = square_sum(part_k[1])
        step = HEAD + 8
        total_q = jnp.concatenate([early[:HEAD], early[step : step + HEAD]], axis=0)
        total_gain = jnp.concatenate([early[HEAD], early[step + HEAD]], axis=0)
        total_k = jnp.concatenate([early[2 * step :], last], axis=0)
    else:

        def in_order(parts):
            spread = [None] * heads
            for g in range(groups):
                for i in range(GROUP):
                    spread[head_of(g, i, groups)] = parts[g][i]
            return jnp.stack(spread)

        both = in_order(sum_q)
        owned = (
            lax.psum_scatter(both[:, :HEAD].reshape(width, HEAD), "dp", scatter_dimension=0, tiled=True),
            lax.psum_scatter(in_order(sum_k).reshape(width, HEAD), "dp", scatter_dimension=0, tiled=True),
            lax.psum_scatter(both[:, HEAD].reshape(width), "dp", scatter_dimension=0, tiled=True),
        )
        total_q, total_k, total_gain = lax.psum(owned, "seq")
    shape = query_in.shape
    return (
        grad_query.reshape(shape),
        grad_key.reshape(shape),
        grad_value.reshape(shape),
        total_q,
        total_k,
        total_gain,
    )


def solution(mesh):
    split = P("dp", "seq", None)
    return jax.shard_map(
        per_device,
        mesh=mesh,
        in_specs=(split, split, split, split, P(), P(), P()),
        out_specs=(split, split, split, P("dp", None), P("dp", None), P("dp")),
        check_vma=False,
    )
```

```python
import functools

import jax
import jax.numpy as jnp
from jax import lax
from jax.experimental import pallas as pl
from jax.experimental.pallas import tpu as pltpu
from jax.sharding import PartitionSpec as P

HEAD = 128
GROUP = 4
FIRST_VMEM = 64 * 1024 - 1600
NORM_EPS = 1e-05
F32 = jnp.float32
BF16 = jnp.bfloat16


def dot(a, b, ca=1, cb=0):
    return lax.dot_general(a, b, (((ca,), (cb,)), ((), ())), preferred_element_type=F32)


def feature(pre):
    return jnp.where(pre > 0.0, pre + 1.0, jnp.exp(jnp.minimum(pre, 0.0)))


def split_low(value):
    high = value.astype(BF16)
    return high, (value - high.astype(F32)).astype(BF16)


def tril(rows):
    return lax.broadcasted_iota(jnp.int32, (rows, rows), 0) >= lax.broadcasted_iota(
        jnp.int32, (rows, rows), 1
    )


def columns(offset, i):
    at = (2 * i + offset) * HEAD
    return slice(at, at + HEAD)


def place_in_square():
    mine = lax.axis_index("seq")
    return lax.rem(mine, 2), lax.div(mine, 2)


def summed(order, later, first, second):
    if order == "all":
        return [first[i] for i in range(GROUP)]
    at_x, at_y = place_in_square()
    if order == "xy":
        keep_first, keep_second = at_x != later, at_y != later
        return [
            jnp.where(keep_first, first[i], 0.0) + jnp.where(keep_second, second[i], 0.0) for i in range(GROUP)
        ]
    keep_first = at_y != later
    return [jnp.where(keep_first, first[i], 0.0) + second[i] for i in range(GROUP)]


def turn_kernel(later, own, first, out):
    at_x, at_y = place_in_square()
    out[...] = jnp.where(at_y != later, first[...], 0.0) + jnp.where(at_x == later, own[...], 0.0)


def bit_clear(bit):
    return lax.rem(lax.div(lax.axis_index("dp"), bit), 2) == 0


def key_features(key, w_key):
    return [
        [feature(dot(key[:, c], w_key[c, :])).astype(BF16) for c in (columns(offset, i) for i in range(GROUP))]
        for offset in range(2)
    ]


def key_states(low, value, outs):
    for offset in range(2):
        feat_key, state = outs[2 * offset : 2 * offset + 2]
        states = [dot(low[offset][i], value[:, columns(offset, i)], 0, 0) for i in range(GROUP)]
        for i in range(GROUP):
            state[i] = states[i]
            feat_key[i] = low[offset][i]


def key_kernel(key, value, w_key, *outs):
    key_states(key_features(key, w_key), value, outs)


def first_kernel(key, value, w_key, *refs):
    outs, (key_buf, value_buf, w_buf, sems) = refs[:4], refs[4:]
    span = pl.ds(0, key_buf.shape[1])
    copies = [
        pltpu.make_async_copy(key.at[:, span], key_buf, sems.at[0]),
        pltpu.make_async_copy(w_key.at[span, :], w_buf, sems.at[1]),
        pltpu.make_async_copy(value.at[:, span], value_buf, sems.at[2]),
    ]
    for copy in copies:
        copy.start()
    copies[0].wait()
    copies[1].wait()
    low = key_features(key_buf, w_buf)
    copies[2].wait()
    key_states(low, value_buf, outs)


def query_kernel(offset, query, w_query, feat_key, feat_query, attn):
    causal = tril(query.shape[0])
    at = [columns(offset, i) for i in range(GROUP)]
    low = [feature(dot(query[:, c], w_query[c, :])).astype(BF16) for c in at]
    scores = [dot(low[i], feat_key[i], 1, 1) for i in range(GROUP)]
    for i in range(GROUP):
        feat_query[i] = low[i]
        attn[i] = jnp.where(causal, scores[i], 0.0).astype(BF16)


def numer_kernel(offset, order, first, second, feat_query, attn, value, grad, gain, adjoint, low_out, rest_out, ph_out, pl_out, gain_out):
    every = range(GROUP)
    at = [columns(offset, i) for i in every]
    inner = [dot(attn[i], value[:, at[i]]) for i in every]
    prior = summed(order, 0, first, second)
    parts = [split_low(p) for p in prior]
    feat = [feat_query[i] for i in every]
    numer = [inner[i] + dot(feat[i], parts[i][0]) + dot(feat[i], parts[i][1]) for i in every]
    inv = [lax.rsqrt(jnp.mean(n * n, axis=-1, keepdims=True) + NORM_EPS) for n in numer]
    normed = [n * r for n, r in zip(numer, inv)]
    grad_f = [grad[:, c].astype(F32) for c in at]
    scaled = [x * gain[:, c] for x, c in zip(grad_f, at)]
    means = [jnp.mean(x * n, axis=-1, keepdims=True) for x, n in zip(scaled, normed)]
    grads = [split_low(inv[i] * (scaled[i] - normed[i] * means[i])) for i in every]
    states = [dot(feat[i], grads[i][0], 0, 0) for i in every]
    for i in every:
        adjoint[i] = states[i]
        low_out[i], rest_out[i] = grads[i]
        ph_out[i], pl_out[i] = parts[i]
        gain_out[i] = jnp.broadcast_to(jnp.sum(normed[i] * grad_f[i], axis=0, keepdims=True), (8, HEAD))


def query_grad_kernel(offset, numer_low, rest, high, low, feat_key, query, value, w_query, gain, mixed_out, grad_out, weight):
    causal = tril(query.shape[0])
    every = range(GROUP)
    at = [columns(offset, i) for i in every]
    grad_low = [numer_low[i] for i in every]
    slope = [jnp.minimum(feature(dot(query[:, c], w_query[c, :])), 1.0) for c in at]
    raw = [dot(grad_low[i], value[:, at[i]], 1, 1) for i in every]
    mixed = [jnp.where(causal, x, 0.0).astype(BF16) for x in raw]
    grad_fq = [
        dot(mixed[i], feat_key[i])
        + dot(grad_low[i], high[i], 1, 1)
        + dot(grad_low[i], low[i], 1, 1)
        + dot(rest[i], high[i], 1, 1)
        for i in every
    ]
    pre = [(grad_fq[i] * slope[i]).astype(BF16) for i in every]
    sums = [dot(query[:, at[i]], pre[i], 0, 0) for i in every]
    back = [dot(pre[i], w_query[at[i], :], 1, 1) for i in every]
    for i in every:
        mixed_out[i] = mixed[i]
        grad_out[i] = back[i].astype(BF16)
        weight[i, :HEAD, :] = sums[i]
        weight[i, HEAD:, :] = gain[i]


def key_grad_kernel(offset, order, first, second, mixed, feat_query, key, value, w_key, pre_out, lh_out, ll_out, weight):
    every = range(GROUP)
    at = [columns(offset, i) for i in every]
    slope = [jnp.minimum(feature(dot(key[:, c], w_key[c, :])), 1.0) for c in at]
    later = summed(order, 1, first, second)
    parts = [split_low(x) for x in later]
    val = [value[:, c] for c in at]
    grad_fk = [
        dot(mixed[i], feat_query[i], 0, 0) + dot(val[i], parts[i][0], 1, 1) + dot(val[i], parts[i][1], 1, 1)
        for i in every
    ]
    pre = [(grad_fk[i] * slope[i]).astype(BF16) for i in every]
    sums = [dot(key[:, at[i]], pre[i], 0, 0) for i in every]
    for i in every:
        weight[i] = sums[i]
        pre_out[i] = pre[i]
        lh_out[i], ll_out[i] = parts[i]


def value_grad_kernel(offset, attn, numer_low, feat_key, high, low, pre, w_key, key_out, value_out):
    every = range(GROUP)
    feat = [feat_key[i] for i in every]
    grads = [
        dot(attn[i], numer_low[i], 0, 0) + dot(feat[i], high[i]) + dot(feat[i], low[i]) for i in every
    ]
    back = [dot(pre[i], w_key[columns(offset, i), :], 1, 1) for i in every]
    for i in every:
        value_out[i] = grads[i].astype(BF16)
        key_out[i] = back[i].astype(BF16)


def lay_kernel(groups, *refs):
    out, laid, sem = refs[groups:]
    for g in range(groups):
        for i in range(GROUP):
            laid[:, place(g, i)] = refs[g][i]
    copy = pltpu.make_async_copy(laid, out, sem)
    copy.start()
    copy.wait()


def pair_kernel(one, two, out):
    out[...] = one[...] + two[...]


def core_kernel(even, odd, kept, sent):
    first = bit_clear(1)
    for m in range(2):
        for b, part in enumerate((even, odd)):
            one, two = part[2 * m], part[2 * m + 1]
            kept[m, b] = jnp.where(first, one, two)
            sent[m, b] = jnp.where(first, two, one)


def near_kernel(*refs):
    parts, (kept, sent) = refs[:-2], refs[-2:]
    first = bit_clear(2)
    for block in range(2):
        own, theirs = parts[2 * block : 2 * block + 2]
        one, two = own[0] + theirs[0], own[1] + theirs[1]
        kept[block] = jnp.where(first, one, two)
        sent[block] = jnp.where(first, two, one)


def far_kernel(mine, theirs, kept, sent):
    first = bit_clear(4)
    one, two = mine[0] + theirs[0], mine[1] + theirs[1]
    kept[...] = jnp.where(first, one, two)
    sent[...] = jnp.where(first, two, one)


def spread_kernel(*refs):
    (low_own, low_theirs, high_own, high_theirs), outs = refs[:4], refs[4:]
    near, far = bit_clear(2), bit_clear(4)
    for m in range(2):
        low = low_own[m] + low_theirs[m]
        high = high_own[m] + high_theirs[m]
        here, there = jnp.where(far, low, high), jnp.where(far, high, low)
        same = near if m == 0 else jnp.logical_not(near)

        @pl.when(same)
        def _():
            outs[0][...] = here
            outs[2][...] = there

        @pl.when(jnp.logical_not(same))
        def _():
            outs[1][...] = here
            outs[3][...] = there


def gather_kernel(own, near, far, both, out):
    out[...] = (own[...] + near[...]) + (far[...] + both[...])


def halves_kernel(one, two, even, odd):
    even[...] = one[0] + two[0]
    odd[...] = one[1] + two[1]


def both_pairs_kernel(even, even_other, odd, odd_other, even_out, odd_out):
    even_out[...] = even[...] + even_other[...]
    odd_out[...] = odd[...] + odd_other[...]


def total_kernel(*refs):
    query, (key, key_x, key_y, key_d), (out_q, out_k, out_gain) = refs[:4], refs[4:8], refs[8:]
    total_k = (key[...] + key_x[...]) + (key_y[...] + key_d[...])
    for b in range(2):
        total_q = query[2 * b][...] + query[2 * b + 1][...]
        out_q[b * HEAD : (b + 1) * HEAD, :] = total_q[:HEAD, :]
        out_gain[b : b + 1, :] = total_q[HEAD : HEAD + 1, :]
        out_k[b * HEAD : (b + 1) * HEAD, :] = total_k[b]


def head_of(g, i):
    return (g // 2) * 2 * GROUP + 2 * i + g % 2


def place(g, i):
    at = head_of(g, i) * HEAD
    return slice(at, at + HEAD)


class Order:
    def __init__(self):
        self.last = None

    def __call__(self, body, ins, outs, name, scratch=(), to_hbm=False, chain=True, vmem=12 * 1024):
        at = len(ins)
        after = chain and self.last is not None
        if after:
            ins = ins + [(self.last, pl.BlockSpec(memory_space=pl.ANY))]
        inputs, results = len(ins), len(outs)

        def ordered(*refs):
            body(*refs[:at], *refs[inputs : inputs + results], *refs[inputs + results + chain :])
            if chain:
                token = refs[inputs + results]
                token[...] = jnp.zeros_like(token)

        out_specs = [
            pl.BlockSpec(memory_space=pltpu.HBM) if to_hbm else pl.BlockSpec(shape, lambda _, n=len(shape): (0,) * n)
            for shape, _ in outs
        ]
        out_shape = [jax.ShapeDtypeStruct(shape, kind) for shape, kind in outs]
        if chain:
            out_specs.append(pl.BlockSpec((8, HEAD), lambda _: (0, 0)))
            out_shape.append(jax.ShapeDtypeStruct((8, HEAD), F32))
        result = pl.pallas_call(
            ordered,
            grid=(1,),
            in_specs=[spec for _, spec in ins],
            out_specs=out_specs,
            out_shape=out_shape,
            scratch_shapes=list(scratch),
            compiler_params=pltpu.CompilerParams(vmem_limit_bytes=vmem * 1024),
            cost_estimate=pl.CostEstimate(flops=200000000, bytes_accessed=0, transcendentals=0),
            name=name,
        )(*[x for x, _ in ins])
        if chain:
            self.last = result[-1]
            return result[:-1]
        return result


def whole(x):
    return (x, pl.BlockSpec(x.shape, lambda _, n=x.ndim: (0,) * n))


def in_hbm(x):
    return (x, pl.BlockSpec(memory_space=pltpu.HBM))


def scan_generic(value, reverse):
    peers, mine = lax.axis_size("seq"), lax.axis_index("seq")
    everything = lax.all_gather(value, "seq")

    def turn(k, before):
        reached = k > mine if reverse else k < mine
        return before + jnp.where(reached, everything[k], 0.0)

    return lax.fori_loop(0, peers, turn, jnp.zeros_like(value))


def swap(value, axis, bit):
    return lax.ppermute(value, axis, [(i, i ^ bit) for i in range(lax.axis_size(axis))])


def per_device(query_in, key_in, value_in, grad_out, w_query, w_key, norm_gain):
    _, rows, width = query_in.shape
    heads = width // HEAD
    groups = heads // GROUP
    tuned = lax.axis_size("seq") == 4 and lax.axis_size("dp") == 8 and heads == 16
    query, key, value, grad = (x.reshape(rows, width) for x in (query_in, key_in, value_in, grad_out))
    gain = norm_gain.reshape(1, width)
    wide = 2 * GROUP * HEAD

    def cols(x, g):
        return (x, pl.BlockSpec((x.shape[0], wide), lambda _: (0, g // 2)))

    def wrows(x, g):
        return (x, pl.BlockSpec((wide, HEAD), lambda _: (g // 2, 0)))

    def tok(kind):
        return ((GROUP, rows, HEAD), kind)

    def sq(kind):
        return ((GROUP, HEAD, HEAD), kind)

    call = Order()

    def pair(one, two, name):
        (out,) = call(pair_kernel, [whole(one), whole(two)], [(one.shape, F32)], name)
        return out

    feat_k, state, feat_q, attn = {}, {}, {}, {}
    numer, mixed, back_q, sum_q = {}, {}, {}, {}
    pre_k, late_h, late_l, sum_k, back_k, back_v = {}, {}, {}, {}, {}, {}
    first, second, first_back, second_back = {}, {}, {}, {}

    def order_of(g):
        if not tuned:
            return "all"
        return ("xy", "yx")[g % 2]

    def hop_one(value, g, later):
        if not tuned:
            return scan_generic(value, later == 1)
        return swap(value, "seq", 1 if order_of(g) == "xy" else 2)

    def hop_two(value, brought, g, later):
        if not tuned:
            return brought
        if order_of(g) == "xy":
            return swap(pair(value, brought, f"pair_{later}_{g}"), "seq", 2)
        body = functools.partial(turn_kernel, later)
        (out,) = call(body, [whole(value), whole(brought)], [(value.shape, F32)], f"turn_{later}_{g}")
        return swap(out, "seq", 1)

    def key_state(g):
        outs = [tok(BF16), sq(F32)] * 2
        if g == 0:
            scratch = [
                pltpu.VMEM((rows, wide), BF16),
                pltpu.VMEM((rows, wide), BF16),
                pltpu.VMEM((wide, HEAD), BF16),
                pltpu.SemaphoreType.DMA((3,)),
            ]
            inputs = [in_hbm(key), in_hbm(value), in_hbm(w_key)]
            result = call(first_kernel, inputs, outs, "key_state_0", scratch, vmem=FIRST_VMEM)
        else:
            result = call(key_kernel, [cols(key, g), cols(value, g), wrows(w_key, g)], outs, f"key_state_{g}")
        feat_k[g], state[g], feat_k[g + 1], state[g + 1] = result
        for k in (g, g + 1):
            first[k] = hop_one(state[k], k, 0)

    def prior_hop(g):
        second[g] = hop_two(state[g], first[g], g, 0)

    def query_attn(g):
        feat_q[g], attn[g] = call(
            functools.partial(query_kernel, g % 2),
            [cols(query, g), wrows(w_query, g), whole(feat_k[g])],
            [tok(BF16), ((GROUP, rows, rows), BF16)],
            f"query_attn_{g}",
        )

    def numer_state(g):
        numer[g] = call(
            functools.partial(numer_kernel, g % 2, order_of(g)),
            [whole(first[g]), whole(second[g]), whole(feat_q[g]), whole(attn[g]), cols(value, g), cols(grad, g), cols(gain, g)],
            [sq(F32), tok(BF16), tok(BF16), sq(BF16), sq(BF16), ((GROUP, 8, HEAD), F32)],
            f"numer_{g}",
        )
        first_back[g] = hop_one(numer[g][0], g, 1)

    def later_hop(g):
        second_back[g] = hop_two(numer[g][0], first_back[g], g, 1)

    def query_grad(g):
        _, low, rest, ph, pl_, gains = numer[g]
        mixed[g], back_q[g], sum_q[g] = call(
            functools.partial(query_grad_kernel, g % 2),
            [whole(x) for x in (low, rest, ph, pl_, feat_k[g])]
            + [cols(query, g), cols(value, g), wrows(w_query, g), whole(gains)],
            [((GROUP, rows, rows), BF16), tok(BF16), ((GROUP, HEAD + 8, HEAD), F32)],
            f"query_grad_{g}",
        )

    def key_grad(g):
        pre_k[g], late_h[g], late_l[g], sum_k[g] = call(
            functools.partial(key_grad_kernel, g % 2, order_of(g)),
            [whole(first_back[g]), whole(second_back[g]), whole(mixed[g]), whole(feat_q[g])]
            + [cols(key, g), cols(value, g), wrows(w_key, g)],
            [tok(BF16), sq(BF16), sq(BF16), sq(F32)],
            f"key_grad_{g}",
        )

    def value_grad(g):
        back_k[g], back_v[g] = call(
            functools.partial(value_grad_kernel, g % 2),
            [whole(x) for x in (attn[g], numer[g][1], feat_k[g], late_h[g], late_l[g], pre_k[g])] + [wrows(w_key, g)],
            [tok(BF16), tok(BF16)],
            f"value_grad_{g}",
        )

    hops = {}

    def core_hop(b):
        parts = sum_q if b > 1 else sum_k
        parts = [whole(parts[2 * (b % 2)]), whole(parts[2 * (b % 2) + 1])]
        shape = (2, 2) + parts[0][0].shape[1:]
        kept, sent = call(core_kernel, parts, [(shape, F32)] * 2, f"core_{b}")
        hops[b] = (kept, swap(sent, "dp", 1))

    def near_hop(b):
        inputs = [whole(x) for x in hops[2] + hops[3]]
        kept, sent = call(near_kernel, inputs, [(hops[2][0].shape, F32)] * 2, "near")
        hops[2] = (kept, swap(sent, "dp", 2))

    def far_hop(b):
        kept, sent = call(far_kernel, [whole(x) for x in hops[2]], [(hops[2][0].shape[1:], F32)] * 2, "far")
        hops[2] = (kept, swap(sent, "dp", 4))

    def z_hop(b):
        inputs = hops[0] + hops[1]
        own, *sent = call(spread_kernel, [whole(x) for x in inputs], [(inputs[1].shape[1:], F32)] * 4, "spread")
        hops[0] = (own,) + tuple(swap(x, "dp", 2 * bits) for bits, x in enumerate(sent, 1))

    totals = {}

    def square(part):
        return (part,) + tuple(swap(part, "seq", bits) for bits in (1, 2, 3))

    def query_first(_):
        parts = call(halves_kernel, [whole(x) for x in hops[2]], [(hops[2][0].shape[1:], F32)] * 2, "query_sum")
        totals["query"] = [(x, swap(x, "seq", bit)) for bit, x in enumerate(parts, 1)]

    def query_second(_):
        parts = call(
            both_pairs_kernel, [whole(x) for x in sum(totals["query"], ())], [(totals["query"][0][0].shape, F32)] * 2, "query_turn"
        )
        totals["query"] = [(x, swap(x, "seq", 2 - bit)) for bit, x in enumerate(parts)]

    def key_square(_):
        (part,) = call(gather_kernel, [whole(x) for x in hops[0]], [(hops[0][0].shape, F32)], "key_sum")
        totals["key"] = square(part)

    def total(_):
        rows_out = ((2 * HEAD, HEAD), F32)
        totals["q"], totals["k"], totals["gain"] = call(
            total_kernel,
            [whole(x) for x in sum(totals["query"], ()) + totals["key"]],
            [rows_out, rows_out, ((2, HEAD), F32)],
            "total",
        )

    def listed(by_group):
        return [by_group[g] for g in range(groups)]

    laid = {}

    def lay(k):
        parts = (back_q, back_k, back_v)[k]
        (laid[k],) = call(
            functools.partial(lay_kernel, groups),
            [whole(x) for x in listed(parts)],
            [((rows, width), BF16)],
            f"lay_{k}",
            [pltpu.VMEM((rows, width), BF16), pltpu.SemaphoreType.DMA(())],
            True,
        )

    if tuned:
        steps = (
            "K0K2Q0Q1p0p1Q2Q3p2p3N0N1G0G1N2N3a2G2G3",
            "l0l1a3l2l3B2H0H1a0V0V1H2H3a1c2V2V3Z0E0L0L1C0F0L2T0",
        )
        steps = "".join(steps)
    else:
        steps = "".join(f"K{g}" for g in range(0, groups, 2))
        steps += "".join(f"{kind}{g}" for kind in "pQNlGHV" for g in range(groups)) + "L0L1L2"
    does = {
        "K": key_state,
        "p": prior_hop,
        "Q": query_attn,
        "N": numer_state,
        "l": later_hop,
        "G": query_grad,
        "H": key_grad,
        "V": value_grad,
        "L": lay,
        "a": core_hop,
        "B": near_hop,
        "c": far_hop,
        "Z": z_hop,
        "E": query_first,
        "F": query_second,
        "C": key_square,
        "T": total,
    }
    for k in range(0, len(steps), 2):
        does[steps[k]](int(steps[k + 1]))
    if tuned:
        total_q, total_k, total_gain = totals["q"], totals["k"], totals["gain"].reshape(2 * HEAD)
    else:

        def in_order(parts):
            spread = [None] * heads
            for g in range(groups):
                for i in range(GROUP):
                    spread[head_of(g, i)] = parts[g][i]
            return jnp.stack(spread)

        both = in_order(sum_q)
        owned = (
            lax.psum_scatter(both[:, :HEAD].reshape(width, HEAD), "dp", scatter_dimension=0, tiled=True),
            lax.psum_scatter(in_order(sum_k).reshape(width, HEAD), "dp", scatter_dimension=0, tiled=True),
            lax.psum_scatter(both[:, HEAD].reshape(width), "dp", scatter_dimension=0, tiled=True),
        )
        total_q, total_k, total_gain = lax.psum(owned, "seq")
    shape = query_in.shape
    return (
        laid[0].reshape(shape),
        laid[1].reshape(shape),
        laid[2].reshape(shape),
        total_q,
        total_k,
        total_gain,
    )


def solution(mesh):
    split = P("dp", "seq", None)
    return jax.shard_map(
        per_device,
        mesh=mesh,
        in_specs=(split, split, split, split, P(), P(), P()),
        out_specs=(split, split, split, P("dp", None), P("dp", None), P("dp")),
        check_vma=False,
    )
```

```python
import functools

import jax
import jax.numpy as jnp
from jax import lax
from jax.experimental import pallas as pl
from jax.experimental.pallas import tpu as pltpu
from jax.sharding import PartitionSpec as P

HEAD = 128
GROUP = 4
FIRST_VMEM = 64 * 1024 - 4000
NORM_EPS = 1e-05
F32 = jnp.float32
BF16 = jnp.bfloat16


def dot(a, b, ca=1, cb=0):
    return lax.dot_general(a, b, (((ca,), (cb,)), ((), ())), preferred_element_type=F32)


def feature(pre):
    return jnp.where(pre > 0.0, pre + 1.0, jnp.exp(jnp.minimum(pre, 0.0)))


def split_low(value):
    high = value.astype(BF16)
    return high, (value - high.astype(F32)).astype(BF16)


def tril(rows):
    return lax.broadcasted_iota(jnp.int32, (rows, rows), 0) >= lax.broadcasted_iota(
        jnp.int32, (rows, rows), 1
    )


def columns(i):
    return slice(i * HEAD, (i + 1) * HEAD)


def place_in_square():
    mine = lax.axis_index("seq")
    return lax.rem(mine, 2), lax.div(mine, 2)


def summed(order, later, first, second):
    if order == "all":
        return [first[i] for i in range(GROUP)]
    at_x, at_y = place_in_square()
    if order == "xy":
        keep_first, keep_second = at_x != later, at_y != later
        return [
            jnp.where(keep_first, first[i], 0.0) + jnp.where(keep_second, second[i], 0.0) for i in range(GROUP)
        ]
    keep_first = at_y != later
    return [jnp.where(keep_first, first[i], 0.0) + second[i] for i in range(GROUP)]


def turn_kernel(later, own, first, out):
    at_x, at_y = place_in_square()
    out[...] = jnp.where(at_y != later, first[...], 0.0) + jnp.where(at_x == later, own[...], 0.0)


def bit_clear(bit):
    return lax.rem(lax.div(lax.axis_index("dp"), bit), 2) == 0


def key_features(key, w_key):
    return [feature(dot(key[:, c], w_key[c, :])).astype(BF16) for c in map(columns, range(2 * GROUP))]


def key_states(low, value, *outs):
    states = [dot(f, value[:, columns(i)], 0, 0) for i, f in enumerate(low)]
    for g in range(2):
        for i in range(GROUP):
            outs[2 * g][i] = low[g * GROUP + i]
            outs[2 * g + 1][i] = states[g * GROUP + i]


def key_kernel(key, value, w_key, *outs):
    key_states(key_features(key, w_key), value, *outs)


def first_kernel(key, value, w_key, *refs):
    outs, (key_buf, value_buf, w_buf, sems) = refs[:4], refs[4:]
    span = pl.ds(0, key_buf.shape[1])
    copies = [
        pltpu.make_async_copy(key.at[:, span], key_buf, sems.at[0]),
        pltpu.make_async_copy(w_key.at[span, :], w_buf, sems.at[1]),
        pltpu.make_async_copy(value.at[:, span], value_buf, sems.at[2]),
    ]
    for copy in copies:
        copy.start()
    copies[0].wait()
    copies[1].wait()
    low = key_features(key_buf, w_buf)
    copies[2].wait()
    key_states(low, value_buf, *outs)


def query_kernel(query, w_query, feat_key, feat_query, attn):
    causal = tril(query.shape[0])
    at = [columns(i) for i in range(GROUP)]
    low = [feature(dot(query[:, c], w_query[c, :])).astype(BF16) for c in at]
    scores = [dot(low[i], feat_key[i], 1, 1) for i in range(GROUP)]
    for i in range(GROUP):
        feat_query[i] = low[i]
        attn[i] = jnp.where(causal, scores[i], 0.0).astype(BF16)


def numer_kernel(order, first, second, feat_query, attn, value, grad, gain, adjoint, low_out, rest_out, ph_out, pl_out, gain_out):
    every = range(GROUP)
    at = [columns(i) for i in every]
    inner = [dot(attn[i], value[:, at[i]]) for i in every]
    prior = summed(order, 0, first, second)
    parts = [split_low(p) for p in prior]
    feat = [feat_query[i] for i in every]
    numer = [inner[i] + dot(feat[i], parts[i][0]) + dot(feat[i], parts[i][1]) for i in every]
    inv = [lax.rsqrt(jnp.mean(n * n, axis=-1, keepdims=True) + NORM_EPS) for n in numer]
    normed = [n * r for n, r in zip(numer, inv)]
    grad_f = [grad[:, c].astype(F32) for c in at]
    scaled = [x * gain[:, c] for x, c in zip(grad_f, at)]
    means = [jnp.mean(x * n, axis=-1, keepdims=True) for x, n in zip(scaled, normed)]
    grads = [split_low(inv[i] * (scaled[i] - normed[i] * means[i])) for i in every]
    states = [dot(feat[i], grads[i][0], 0, 0) for i in every]
    for i in every:
        adjoint[i] = states[i]
        low_out[i], rest_out[i] = grads[i]
        ph_out[i], pl_out[i] = parts[i]
        gain_out[i] = jnp.broadcast_to(jnp.sum(normed[i] * grad_f[i], axis=0, keepdims=True), (8, HEAD))


def query_grad_kernel(numer_low, rest, high, low, feat_key, query, value, w_query, gain, mixed_out, grad_out, weight):
    causal = tril(query.shape[0])
    every = range(GROUP)
    at = [columns(i) for i in every]
    grad_low = [numer_low[i] for i in every]
    slope = [jnp.minimum(feature(dot(query[:, c], w_query[c, :])), 1.0) for c in at]
    raw = [dot(grad_low[i], value[:, at[i]], 1, 1) for i in every]
    mixed = [jnp.where(causal, x, 0.0).astype(BF16) for x in raw]
    grad_fq = [
        dot(mixed[i], feat_key[i])
        + dot(grad_low[i], high[i], 1, 1)
        + dot(grad_low[i], low[i], 1, 1)
        + dot(rest[i], high[i], 1, 1)
        for i in every
    ]
    pre = [(grad_fq[i] * slope[i]).astype(BF16) for i in every]
    sums = [dot(query[:, at[i]], pre[i], 0, 0) for i in every]
    back = [dot(pre[i], w_query[at[i], :], 1, 1) for i in every]
    for i in every:
        mixed_out[i] = mixed[i]
        grad_out[i] = back[i].astype(BF16)
        weight[i, :HEAD, :] = sums[i]
        weight[i, HEAD:, :] = gain[i]


def key_grad_kernel(order, first, second, mixed, feat_query, key, value, w_key, pre_out, lh_out, ll_out, weight):
    every = range(GROUP)
    at = [columns(i) for i in every]
    slope = [jnp.minimum(feature(dot(key[:, c], w_key[c, :])), 1.0) for c in at]
    later = summed(order, 1, first, second)
    parts = [split_low(x) for x in later]
    val = [value[:, c] for c in at]
    grad_fk = [
        dot(mixed[i], feat_query[i], 0, 0) + dot(val[i], parts[i][0], 1, 1) + dot(val[i], parts[i][1], 1, 1)
        for i in every
    ]
    pre = [(grad_fk[i] * slope[i]).astype(BF16) for i in every]
    sums = [dot(key[:, at[i]], pre[i], 0, 0) for i in every]
    for i in every:
        weight[i] = sums[i]
        pre_out[i] = pre[i]
        lh_out[i], ll_out[i] = parts[i]


def value_grad_kernel(attn, numer_low, feat_key, high, low, pre, w_key, key_out, value_out):
    every = range(GROUP)
    feat = [feat_key[i] for i in every]
    grads = [
        dot(attn[i], numer_low[i], 0, 0) + dot(feat[i], high[i]) + dot(feat[i], low[i]) for i in every
    ]
    back = [dot(pre[i], w_key[columns(i), :], 1, 1) for i in every]
    for i in every:
        value_out[i] = grads[i].astype(BF16)
        key_out[i] = back[i].astype(BF16)


def lay_kernel(groups, *refs):
    out, laid, sem = refs[groups:]
    for g in range(groups):
        for i in range(GROUP):
            laid[:, place(g, i)] = refs[g][i]
    copy = pltpu.make_async_copy(laid, out, sem)
    copy.start()
    copy.wait()


def pair_kernel(one, two, out):
    out[...] = one[...] + two[...]


def core_kernel(low, high, *refs):
    if len(refs) == 5:
        one, two, kept, *sent, total = refs
        total[...] = one[...] + two[...]
    else:
        kept, *sent = refs
    first = bit_clear(1)
    for m, part in enumerate((low, high)):
        for b in range(2):
            one, two = part[b], part[2 + b]
            kept[m, b] = jnp.where(first, one, two)
            out = jnp.where(first, two, one)
            if len(sent) == 2:
                sent[m][b] = out
            else:
                sent[0][m, b] = out


def far_kernel(low, own, theirs, kept, sent):
    first = bit_clear(4)
    high = own[...] + theirs[...]
    kept[...] = jnp.where(first, low[...], high)
    sent[...] = jnp.where(first, high, low[...])


def near_kernel(mine, theirs, kept, *sent):
    first = bit_clear(2)
    one, two = mine[0] + theirs[0], mine[1] + theirs[1]
    kept[...] = jnp.where(first, one, two)
    out = jnp.where(first, two, one)
    for b in range(2):
        sent[b][...] = out[b]


def spread_kernel(*refs):
    parts, outs = refs[:6], refs[6:]
    near, far = bit_clear(2), bit_clear(4)
    for m in range(2):
        low = parts[0][m] + parts[1 + m][...]
        high = parts[3][m] + parts[4 + m][...]
        here, there = jnp.where(far, low, high), jnp.where(far, high, low)
        same = near if m == 0 else jnp.logical_not(near)

        @pl.when(same)
        def _():
            outs[0][...] = here
            outs[2][...] = there

        @pl.when(jnp.logical_not(same))
        def _():
            outs[1][...] = here
            outs[3][...] = there


def gather_kernel(own, near, far, both, out):
    out[...] = (own[...] + near[...]) + (far[...] + both[...])


def halves_kernel(own, even_other, odd_other, even, odd):
    even[...] = own[0] + even_other[...]
    odd[...] = own[1] + odd_other[...]


def both_pairs_kernel(even, even_other, odd, odd_other, even_out, odd_out):
    even_out[...] = even[...] + even_other[...]
    odd_out[...] = odd[...] + odd_other[...]


def total_kernel(*refs):
    query, (key, key_x, key_y, key_d), (out_q, out_k, out_gain) = refs[:4], refs[4:8], refs[8:]
    total_k = (key[...] + key_x[...]) + (key_y[...] + key_d[...])
    for b in range(2):
        total_q = query[2 * b][...] + query[2 * b + 1][...]
        out_q[b * HEAD : (b + 1) * HEAD, :] = total_q[:HEAD, :]
        out_gain[b : b + 1, :] = total_q[HEAD : HEAD + 1, :]
        out_k[b * HEAD : (b + 1) * HEAD, :] = total_k[b]


def place(g, i):
    at = (g * GROUP + i) * HEAD
    return slice(at, at + HEAD)


class Order:
    def __init__(self):
        self.last = None

    def __call__(self, body, ins, outs, name, scratch=(), to_hbm=False, to_vmem=False, chain=True, vmem=12 * 1024):
        at = len(ins)
        after = chain and self.last is not None
        if after:
            ins = ins + [(self.last, pl.BlockSpec(memory_space=pl.ANY))]
        inputs, results = len(ins), len(outs)

        def ordered(*refs):
            body(*refs[:at], *refs[inputs : inputs + results], *refs[inputs + results + chain :])
            if chain:
                token = refs[inputs + results]
                token[...] = jnp.zeros_like(token)

        out_specs = [
            pl.BlockSpec(memory_space=pltpu.HBM) if to_hbm else pl.BlockSpec(shape, lambda _, n=len(shape): (0,) * n)
            for shape, _ in outs
        ]
        out_shape = [jax.ShapeDtypeStruct(shape, kind) for shape, kind in outs]
        if to_vmem:
            out_specs = [pl.BlockSpec(memory_space=pltpu.VMEM) for _ in outs]
            out_shape = [pltpu.VMEM(shape, kind) for shape, kind in outs]
        if chain and to_vmem:
            out_specs.append(pl.BlockSpec(memory_space=pltpu.VMEM))
            out_shape.append(pltpu.VMEM((8, HEAD), F32))
        elif chain:
            out_specs.append(pl.BlockSpec((8, HEAD), lambda _: (0, 0)))
            out_shape.append(jax.ShapeDtypeStruct((8, HEAD), F32))
        result = pl.pallas_call(
            ordered,
            grid=(1,),
            in_specs=[spec for _, spec in ins],
            out_specs=out_specs,
            out_shape=out_shape,
            scratch_shapes=list(scratch),
            compiler_params=pltpu.CompilerParams(vmem_limit_bytes=vmem * 1024),
            cost_estimate=pl.CostEstimate(flops=200000000, bytes_accessed=0, transcendentals=0),
            name=name,
        )(*[x for x, _ in ins])
        if chain:
            self.last = result[-1]
            return result[:-1]
        return result


def whole(x):
    return (x, pl.BlockSpec(x.shape, lambda _, n=x.ndim: (0,) * n))


def in_hbm(x):
    return (x, pl.BlockSpec(memory_space=pltpu.HBM))


def scan_generic(value, reverse):
    peers, mine = lax.axis_size("seq"), lax.axis_index("seq")
    everything = lax.all_gather(value, "seq")

    def turn(k, before):
        reached = k > mine if reverse else k < mine
        return before + jnp.where(reached, everything[k], 0.0)

    return lax.fori_loop(0, peers, turn, jnp.zeros_like(value))


def swap(value, axis, bit):
    return lax.ppermute(value, axis, [(i, i ^ bit) for i in range(lax.axis_size(axis))])


def per_device(query_in, key_in, value_in, grad_out, w_query, w_key, norm_gain):
    _, rows, width = query_in.shape
    heads = width // HEAD
    groups = heads // GROUP
    tuned = lax.axis_size("seq") == 4 and lax.axis_size("dp") == 8 and heads == 16
    query, key, value, grad = (x.reshape(rows, width) for x in (query_in, key_in, value_in, grad_out))
    gain = norm_gain.reshape(1, width)
    wide = GROUP * HEAD

    def cols(x, g):
        return (x, pl.BlockSpec((x.shape[0], wide), lambda _: (0, g)))

    def wrows(x, g):
        return (x, pl.BlockSpec((wide, HEAD), lambda _: (g, 0)))

    def tok(kind):
        return ((GROUP, rows, HEAD), kind)

    def sq(kind):
        return ((GROUP, HEAD, HEAD), kind)

    call = Order()

    def pair(one, two, name):
        (out,) = call(pair_kernel, [whole(one), whole(two)], [(one.shape, F32)], name)
        return out

    feat_k, state, feat_q, attn = {}, {}, {}, {}
    numer, mixed, back_q, sum_q = {}, {}, {}, {}
    pre_k, late_h, late_l, sum_k, back_k, back_v = {}, {}, {}, {}, {}, {}
    first, second, first_back, second_back = {}, {}, {}, {}

    def order_of(g):
        if not tuned:
            return "all"
        return ("xy", "yx")[g % 2]

    def hop_one(value, g, later):
        if not tuned:
            return scan_generic(value, later == 1)
        return swap(value, "seq", 1 if order_of(g) == "xy" else 2)

    def hop_two(value, brought, g, later):
        if not tuned:
            return brought
        if order_of(g) == "xy":
            return swap(pair(value, brought, f"pair_{later}_{g}"), "seq", 2)
        body = functools.partial(turn_kernel, later)
        (out,) = call(body, [whole(value), whole(brought)], [(value.shape, F32)], f"turn_{later}_{g}")
        return swap(out, "seq", 1)

    def key_state(g):
        outs = [tok(BF16), sq(F32)] * 2
        pair_wide = 2 * wide
        if g == 0:
            scratch = [
                pltpu.VMEM((rows, pair_wide), BF16),
                pltpu.VMEM((rows, pair_wide), BF16),
                pltpu.VMEM((pair_wide, HEAD), BF16),
                pltpu.SemaphoreType.DMA((3,)),
            ]
            inputs = [in_hbm(key), in_hbm(value), in_hbm(w_key)]
            result = call(first_kernel, inputs, outs, "key_state_first", scratch, to_vmem=True, vmem=FIRST_VMEM)
        else:
            by_cols = pl.BlockSpec((rows, pair_wide), lambda _: (0, g // 2))
            by_rows = pl.BlockSpec((pair_wide, HEAD), lambda _: (g // 2, 0))
            result = call(key_kernel, [(key, by_cols), (value, by_cols), (w_key, by_rows)], outs, f"key_state_{g}")
        feat_k[g], state[g], feat_k[g + 1], state[g + 1] = result
        for k in (g, g + 1):
            first[k] = hop_one(state[k], k, 0)

    def prior_hop(g):
        second[g] = hop_two(state[g], first[g], g, 0)

    def query_attn(g):
        feat_q[g], attn[g] = call(
            query_kernel,
            [cols(query, g), wrows(w_query, g), whole(feat_k[g])],
            [tok(BF16), ((GROUP, rows, rows), BF16)],
            f"query_attn_{g}",
        )

    def numer_state(g):
        numer[g] = call(
            functools.partial(numer_kernel, order_of(g)),
            [whole(first[g]), whole(second[g]), whole(feat_q[g]), whole(attn[g]), cols(value, g), cols(grad, g), cols(gain, g)],
            [sq(F32), tok(BF16), tok(BF16), sq(BF16), sq(BF16), ((GROUP, 8, HEAD), F32)],
            f"numer_{g}",
        )
        first_back[g] = hop_one(numer[g][0], g, 1)

    def later_hop(g):
        second_back[g] = hop_two(numer[g][0], first_back[g], g, 1)

    def query_grad(g):
        _, low, rest, ph, pl_, gains = numer[g]
        mixed[g], back_q[g], sum_q[g] = call(
            query_grad_kernel,
            [whole(x) for x in (low, rest, ph, pl_, feat_k[g])]
            + [cols(query, g), cols(value, g), wrows(w_query, g), whole(gains)],
            [((GROUP, rows, rows), BF16), tok(BF16), ((GROUP, HEAD + 8, HEAD), F32)],
            f"query_grad_{g}",
        )

    def key_grad(g):
        pre_k[g], late_h[g], late_l[g], sum_k[g] = call(
            functools.partial(key_grad_kernel, order_of(g)),
            [whole(first_back[g]), whole(second_back[g]), whole(mixed[g]), whole(feat_q[g])]
            + [cols(key, g), cols(value, g), wrows(w_key, g)],
            [tok(BF16), sq(BF16), sq(BF16), sq(F32)],
            f"key_grad_{g}",
        )

    def value_grad(g):
        back_k[g], back_v[g] = call(
            value_grad_kernel,
            [whole(x) for x in (attn[g], numer[g][1], feat_k[g], late_h[g], late_l[g], pre_k[g])] + [wrows(w_key, g)],
            [tok(BF16), tok(BF16)],
            f"value_grad_{g}",
        )

    hops = {}

    def core_hop(b):
        parts = sum_q if b > 1 else sum_k
        inputs = [whole(parts[2 * (b % 2)]), whole(parts[2 * (b % 2) + 1])]
        shape = (2,) + parts[0].shape[1:]
        both = ((2,) + shape, F32)
        if b == 2:
            kept, sent = call(core_kernel, inputs, [both, both], "core_2")
            hops[b] = (kept, swap(sent, "dp", 1))
        elif b == 3:
            kept, sent, total = call(core_kernel, inputs + [whole(x) for x in hops[2]], [both] * 3, "core_3")
            hops[2] = (total, kept, swap(sent, "dp", 1))
        else:
            kept, *sent = call(core_kernel, inputs, [both, (shape, F32), (shape, F32)], f"core_{b}")
            hops[b] = (kept,) + tuple(swap(x, "dp", 1) for x in sent)

    def far_hop(_):
        kept, sent = call(far_kernel, [whole(x) for x in hops[2]], [(hops[2][0].shape, F32)] * 2, "far")
        hops[2] = (kept, swap(sent, "dp", 4))

    def near_hop(_):
        shape = hops[2][0].shape[1:]
        outs = [(shape, F32), (shape[1:], F32), (shape[1:], F32)]
        kept, *sent = call(near_kernel, [whole(x) for x in hops[2]], outs, "near")
        hops[2] = (kept,) + tuple(swap(x, "dp", 2) for x in sent)

    def z_hop(b):
        inputs = hops[0] + hops[1]
        own, *sent = call(spread_kernel, [whole(x) for x in inputs], [(inputs[1].shape, F32)] * 4, "spread")
        hops[0] = (own,) + tuple(swap(x, "dp", 2 * bits) for bits, x in enumerate(sent, 1))

    totals = {}

    def square(part):
        return (part,) + tuple(swap(part, "seq", bits) for bits in (1, 2, 3))

    def query_first(_):
        parts = call(halves_kernel, [whole(x) for x in hops[2]], [(hops[2][1].shape, F32)] * 2, "query_sum")
        totals["query"] = [(x, swap(x, "seq", bit)) for bit, x in enumerate(parts, 1)]

    def query_second(_):
        parts = call(
            both_pairs_kernel, [whole(x) for x in sum(totals["query"], ())], [(totals["query"][0][0].shape, F32)] * 2, "query_turn"
        )
        totals["query"] = [(x, swap(x, "seq", 2 - bit)) for bit, x in enumerate(parts)]

    def key_square(_):
        (part,) = call(gather_kernel, [whole(x) for x in hops[0]], [(hops[0][0].shape, F32)], "key_sum")
        totals["key"] = square(part)

    def total(_):
        rows_out = ((2 * HEAD, HEAD), F32)
        totals["q"], totals["k"], totals["gain"] = call(
            total_kernel,
            [whole(x) for x in sum(totals["query"], ()) + totals["key"]],
            [rows_out, rows_out, ((2, HEAD), F32)],
            "total",
        )

    def listed(by_group):
        return [by_group[g] for g in range(groups)]

    laid = {}

    def lay(k):
        parts = (back_q, back_k, back_v)[k]
        (laid[k],) = call(
            functools.partial(lay_kernel, groups),
            [whole(x) for x in listed(parts)],
            [((rows, width), BF16)],
            f"lay_{k}",
            [pltpu.VMEM((rows, width), BF16), pltpu.SemaphoreType.DMA(())],
            True,
        )

    if tuned:
        steps = (
            "K0K2Q0Q1p1p0Q2Q3p3p2N0N1G0G1N2N3a2G2G3",
            "l0l1a3l2l3B2H0H1a0V0V1H2H3a1V2V3Z0c2L0L1E0C0F0L2T0",
        )
        steps = "".join(steps)
    else:
        steps = "".join(f"K{g}" for g in range(0, groups, 2))
        steps += "".join(f"{kind}{g}" for kind in "pQNlGHV" for g in range(groups)) + "L0L1L2"
    does = {
        "K": key_state,
        "p": prior_hop,
        "Q": query_attn,
        "N": numer_state,
        "l": later_hop,
        "G": query_grad,
        "H": key_grad,
        "V": value_grad,
        "L": lay,
        "a": core_hop,
        "B": far_hop,
        "c": near_hop,
        "Z": z_hop,
        "E": query_first,
        "F": query_second,
        "C": key_square,
        "T": total,
    }
    for k in range(0, len(steps), 2):
        does[steps[k]](int(steps[k + 1]))
    if tuned:
        total_q, total_k, total_gain = totals["q"], totals["k"], totals["gain"].reshape(2 * HEAD)
    else:

        def in_order(parts):
            return jnp.concatenate(listed(parts), axis=0)

        both = in_order(sum_q)
        owned = (
            lax.psum_scatter(both[:, :HEAD].reshape(width, HEAD), "dp", scatter_dimension=0, tiled=True),
            lax.psum_scatter(in_order(sum_k).reshape(width, HEAD), "dp", scatter_dimension=0, tiled=True),
            lax.psum_scatter(both[:, HEAD].reshape(width), "dp", scatter_dimension=0, tiled=True),
        )
        total_q, total_k, total_gain = lax.psum(owned, "seq")
    shape = query_in.shape
    return (
        laid[0].reshape(shape),
        laid[1].reshape(shape),
        laid[2].reshape(shape),
        total_q,
        total_k,
        total_gain,
    )


def solution(mesh):
    split = P("dp", "seq", None)
    return jax.shard_map(
        per_device,
        mesh=mesh,
        in_specs=(split, split, split, split, P(), P(), P()),
        out_specs=(split, split, split, P("dp", None), P("dp", None), P("dp")),
        check_vma=False,
    )
```

```python
import functools

import jax
import jax.numpy as jnp
from jax import lax
from jax.experimental import pallas as pl
from jax.experimental.pallas import tpu as pltpu
from jax.sharding import PartitionSpec as P

HEAD = 128
GROUP = 4
KEY_VMEM = (64 * 1024 - 4000, 64 * 1024 - 10000)
NORM_EPS = 1e-05
F32 = jnp.float32
BF16 = jnp.bfloat16


def dot(a, b, ca=1, cb=0):
    return lax.dot_general(a, b, (((ca,), (cb,)), ((), ())), preferred_element_type=F32)


def feature(pre):
    return jnp.where(pre > 0.0, pre + 1.0, jnp.exp(jnp.minimum(pre, 0.0)))


def split_low(value):
    high = value.astype(BF16)
    return high, (value - high.astype(F32)).astype(BF16)


def tril(rows):
    return lax.broadcasted_iota(jnp.int32, (rows, rows), 0) >= lax.broadcasted_iota(
        jnp.int32, (rows, rows), 1
    )


def columns(i):
    return slice(i * HEAD, (i + 1) * HEAD)


def place_in_square():
    mine = lax.axis_index("seq")
    return lax.rem(mine, 2), lax.div(mine, 2)


def summed(order, later, first, second):
    if order == "all":
        return [first[i] for i in range(GROUP)]
    at_x, at_y = place_in_square()
    if order == "xy":
        keep_first, keep_second = at_x != later, at_y != later
        return [
            jnp.where(keep_first, first[i], 0.0) + jnp.where(keep_second, second[i], 0.0) for i in range(GROUP)
        ]
    keep_first = at_y != later
    return [jnp.where(keep_first, first[i], 0.0) + second[i] for i in range(GROUP)]


def turn_kernel(later, own, first, out):
    at_x, at_y = place_in_square()
    out[...] = jnp.where(at_y != later, first[...], 0.0) + jnp.where(at_x == later, own[...], 0.0)


def bit_clear(bit):
    return lax.rem(lax.div(lax.axis_index("dp"), bit), 2) == 0


def key_features(key, w_key):
    return [feature(dot(key[:, c], w_key[c, :])).astype(BF16) for c in map(columns, range(2 * GROUP))]


def key_states(low, value, *outs):
    states = [dot(f, value[:, columns(i)], 0, 0) for i, f in enumerate(low)]
    for g in range(2):
        for i in range(GROUP):
            outs[2 * g][i] = low[g * GROUP + i]
            outs[2 * g + 1][i] = states[g * GROUP + i]


def key_kernel(block, key, value, w_key, *refs):
    outs, (key_buf, value_buf, w_buf, sems) = refs[:4], refs[4:]
    span = pl.ds(block * key_buf.shape[1], key_buf.shape[1])
    copies = [
        pltpu.make_async_copy(key.at[:, span], key_buf, sems.at[0]),
        pltpu.make_async_copy(w_key.at[span, :], w_buf, sems.at[1]),
        pltpu.make_async_copy(value.at[:, span], value_buf, sems.at[2]),
    ]
    for copy in copies:
        copy.start()
    copies[0].wait()
    copies[1].wait()
    low = key_features(key_buf, w_buf)
    copies[2].wait()
    key_states(low, value_buf, *outs)


def query_kernel(query, w_query, feat_key, feat_query, attn):
    causal = tril(query.shape[0])
    at = [columns(i) for i in range(GROUP)]
    low = [feature(dot(query[:, c], w_query[c, :])).astype(BF16) for c in at]
    scores = [dot(low[i], feat_key[i], 1, 1) for i in range(GROUP)]
    for i in range(GROUP):
        feat_query[i] = low[i]
        attn[i] = jnp.where(causal, scores[i], 0.0).astype(BF16)


def numer_kernel(order, first, second, feat_query, attn, value, grad, gain, adjoint, low_out, rest_out, ph_out, pl_out, gain_out):
    every = range(GROUP)
    at = [columns(i) for i in every]
    inner = [dot(attn[i], value[:, at[i]]) for i in every]
    prior = summed(order, 0, first, second)
    parts = [split_low(p) for p in prior]
    feat = [feat_query[i] for i in every]
    numer = [inner[i] + dot(feat[i], parts[i][0]) + dot(feat[i], parts[i][1]) for i in every]
    inv = [lax.rsqrt(jnp.mean(n * n, axis=-1, keepdims=True) + NORM_EPS) for n in numer]
    normed = [n * r for n, r in zip(numer, inv)]
    grad_f = [grad[:, c].astype(F32) for c in at]
    scaled = [x * gain[:, c] for x, c in zip(grad_f, at)]
    means = [jnp.mean(x * n, axis=-1, keepdims=True) for x, n in zip(scaled, normed)]
    grads = [split_low(inv[i] * (scaled[i] - normed[i] * means[i])) for i in every]
    states = [dot(feat[i], grads[i][0], 0, 0) for i in every]
    for i in every:
        adjoint[i] = states[i]
        low_out[i], rest_out[i] = grads[i]
        ph_out[i], pl_out[i] = parts[i]
        gain_out[i] = jnp.broadcast_to(jnp.sum(normed[i] * grad_f[i], axis=0, keepdims=True), (8, HEAD))


def query_grad_kernel(numer_low, rest, high, low, feat_key, query, value, w_query, gain, mixed_out, grad_out, weight):
    causal = tril(query.shape[0])
    every = range(GROUP)
    at = [columns(i) for i in every]
    grad_low = [numer_low[i] for i in every]
    slope = [jnp.minimum(feature(dot(query[:, c], w_query[c, :])), 1.0) for c in at]
    raw = [dot(grad_low[i], value[:, at[i]], 1, 1) for i in every]
    mixed = [jnp.where(causal, x, 0.0).astype(BF16) for x in raw]
    grad_fq = [
        dot(mixed[i], feat_key[i])
        + dot(grad_low[i], high[i], 1, 1)
        + dot(grad_low[i], low[i], 1, 1)
        + dot(rest[i], high[i], 1, 1)
        for i in every
    ]
    pre = [(grad_fq[i] * slope[i]).astype(BF16) for i in every]
    sums = [dot(query[:, at[i]], pre[i], 0, 0) for i in every]
    back = [dot(pre[i], w_query[at[i], :], 1, 1) for i in every]
    for i in every:
        mixed_out[i] = mixed[i]
        grad_out[i] = back[i].astype(BF16)
        weight[i, :HEAD, :] = sums[i]
        weight[i, HEAD:, :] = gain[i]


def key_grad_kernel(order, first, second, mixed, feat_query, key, value, w_key, pre_out, lh_out, ll_out, weight):
    every = range(GROUP)
    at = [columns(i) for i in every]
    slope = [jnp.minimum(feature(dot(key[:, c], w_key[c, :])), 1.0) for c in at]
    later = summed(order, 1, first, second)
    parts = [split_low(x) for x in later]
    val = [value[:, c] for c in at]
    grad_fk = [
        dot(mixed[i], feat_query[i], 0, 0) + dot(val[i], parts[i][0], 1, 1) + dot(val[i], parts[i][1], 1, 1)
        for i in every
    ]
    pre = [(grad_fk[i] * slope[i]).astype(BF16) for i in every]
    sums = [dot(key[:, at[i]], pre[i], 0, 0) for i in every]
    for i in every:
        weight[i] = sums[i]
        pre_out[i] = pre[i]
        lh_out[i], ll_out[i] = parts[i]


def value_grad_kernel(attn, numer_low, feat_key, high, low, pre, w_key, key_out, value_out):
    every = range(GROUP)
    feat = [feat_key[i] for i in every]
    grads = [
        dot(attn[i], numer_low[i], 0, 0) + dot(feat[i], high[i]) + dot(feat[i], low[i]) for i in every
    ]
    back = [dot(pre[i], w_key[columns(i), :], 1, 1) for i in every]
    for i in every:
        value_out[i] = grads[i].astype(BF16)
        key_out[i] = back[i].astype(BF16)


def lay_kernel(groups, *refs):
    out, laid, sem = refs[groups:]
    for g in range(groups):
        for i in range(GROUP):
            laid[:, place(g, i)] = refs[g][i]
    copy = pltpu.make_async_copy(laid, out, sem)
    copy.start()
    copy.wait()


def pair_kernel(one, two, out):
    out[...] = one[...] + two[...]


def core_kernel(low, high, *refs):
    if len(refs) == 5:
        one, two, kept, *sent, total = refs
        total[...] = one[...] + two[...]
    else:
        kept, *sent = refs
    first = bit_clear(1)
    for m, part in enumerate((low, high)):
        for b in range(2):
            one, two = part[b], part[2 + b]
            kept[m, b] = jnp.where(first, one, two)
            out = jnp.where(first, two, one)
            if len(sent) == 2:
                sent[m][b] = out
            else:
                sent[0][m, b] = out


def far_kernel(low, own, theirs, kept, sent):
    first = bit_clear(4)
    high = own[...] + theirs[...]
    kept[...] = jnp.where(first, low[...], high)
    sent[...] = jnp.where(first, high, low[...])


def near_kernel(mine, theirs, kept, *sent):
    first = bit_clear(2)
    one, two = mine[0] + theirs[0], mine[1] + theirs[1]
    kept[...] = jnp.where(first, one, two)
    out = jnp.where(first, two, one)
    for b in range(2):
        sent[b][...] = out[b]


def spread_kernel(*refs):
    parts, outs = refs[:6], refs[6:]
    near, far = bit_clear(2), bit_clear(4)
    for m in range(2):
        low = parts[0][m] + parts[1 + m][...]
        high = parts[3][m] + parts[4 + m][...]
        here, there = jnp.where(far, low, high), jnp.where(far, high, low)
        same = near if m == 0 else jnp.logical_not(near)

        @pl.when(same)
        def _():
            outs[0][...] = here
            outs[2][...] = there

        @pl.when(jnp.logical_not(same))
        def _():
            outs[1][...] = here
            outs[3][...] = there


def gather_kernel(own, near, far, both, out):
    out[...] = (own[...] + near[...]) + (far[...] + both[...])


def halves_kernel(own, even_other, odd_other, even, odd):
    even[...] = own[0] + even_other[...]
    odd[...] = own[1] + odd_other[...]


def both_pairs_kernel(even, even_other, odd, odd_other, even_out, odd_out):
    even_out[...] = even[...] + even_other[...]
    odd_out[...] = odd[...] + odd_other[...]


def key_total_kernel(key, key_x, key_y, key_d, out):
    total = (key[...] + key_x[...]) + (key_y[...] + key_d[...])
    for b in range(2):
        out[b * HEAD : (b + 1) * HEAD, :] = total[b]


def query_total_kernel(even, even_other, odd, odd_other, out, out_gain):
    for b, (one, two) in enumerate(((even, even_other), (odd, odd_other))):
        total = one[...] + two[...]
        out[b * HEAD : (b + 1) * HEAD, :] = total[:HEAD, :]
        out_gain[b : b + 1, :] = total[HEAD : HEAD + 1, :]


def place(g, i):
    at = (g * GROUP + i) * HEAD
    return slice(at, at + HEAD)


class Order:
    def __init__(self):
        self.last = None

    def __call__(self, body, ins, outs, name, scratch=(), to_hbm=False, to_vmem=False, chain=True, vmem=12 * 1024):
        at = len(ins)
        after = chain and self.last is not None
        if after:
            ins = ins + [(self.last, pl.BlockSpec(memory_space=pl.ANY))]
        inputs, results = len(ins), len(outs)

        def ordered(*refs):
            body(*refs[:at], *refs[inputs : inputs + results], *refs[inputs + results + chain :])
            if chain:
                token = refs[inputs + results]
                token[...] = jnp.zeros_like(token)

        out_specs = [
            pl.BlockSpec(memory_space=pltpu.HBM) if to_hbm else pl.BlockSpec(shape, lambda _, n=len(shape): (0,) * n)
            for shape, _ in outs
        ]
        out_shape = [jax.ShapeDtypeStruct(shape, kind) for shape, kind in outs]
        if to_vmem:
            out_specs = [pl.BlockSpec(memory_space=pltpu.VMEM) for _ in outs]
            out_shape = [pltpu.VMEM(shape, kind) for shape, kind in outs]
        if chain and to_vmem:
            out_specs.append(pl.BlockSpec(memory_space=pltpu.VMEM))
            out_shape.append(pltpu.VMEM((8, HEAD), F32))
        elif chain:
            out_specs.append(pl.BlockSpec((8, HEAD), lambda _: (0, 0)))
            out_shape.append(jax.ShapeDtypeStruct((8, HEAD), F32))
        result = pl.pallas_call(
            ordered,
            grid=(1,),
            in_specs=[spec for _, spec in ins],
            out_specs=out_specs,
            out_shape=out_shape,
            scratch_shapes=list(scratch),
            compiler_params=pltpu.CompilerParams(vmem_limit_bytes=vmem * 1024),
            cost_estimate=pl.CostEstimate(flops=200000000, bytes_accessed=0, transcendentals=0),
            name=name,
        )(*[x for x, _ in ins])
        if chain:
            self.last = result[-1]
            return result[:-1]
        return result


def whole(x):
    return (x, pl.BlockSpec(x.shape, lambda _, n=x.ndim: (0,) * n))


def in_hbm(x):
    return (x, pl.BlockSpec(memory_space=pltpu.HBM))


def scan_generic(value, reverse):
    peers, mine = lax.axis_size("seq"), lax.axis_index("seq")
    everything = lax.all_gather(value, "seq")

    def turn(k, before):
        reached = k > mine if reverse else k < mine
        return before + jnp.where(reached, everything[k], 0.0)

    return lax.fori_loop(0, peers, turn, jnp.zeros_like(value))


def swap(value, axis, bit):
    return lax.ppermute(value, axis, [(i, i ^ bit) for i in range(lax.axis_size(axis))])


def per_device(query_in, key_in, value_in, grad_out, w_query, w_key, norm_gain):
    _, rows, width = query_in.shape
    heads = width // HEAD
    groups = heads // GROUP
    tuned = lax.axis_size("seq") == 4 and lax.axis_size("dp") == 8 and heads == 16
    query, key, value, grad = (x.reshape(rows, width) for x in (query_in, key_in, value_in, grad_out))
    gain = norm_gain.reshape(1, width)
    wide = GROUP * HEAD

    def cols(x, g):
        return (x, pl.BlockSpec((x.shape[0], wide), lambda _: (0, g)))

    def wrows(x, g):
        return (x, pl.BlockSpec((wide, HEAD), lambda _: (g, 0)))

    def tok(kind):
        return ((GROUP, rows, HEAD), kind)

    def sq(kind):
        return ((GROUP, HEAD, HEAD), kind)

    call = Order()

    def pair(one, two, name):
        (out,) = call(pair_kernel, [whole(one), whole(two)], [(one.shape, F32)], name)
        return out

    feat_k, state, feat_q, attn = {}, {}, {}, {}
    numer, mixed, back_q, sum_q = {}, {}, {}, {}
    pre_k, late_h, late_l, sum_k, back_k, back_v = {}, {}, {}, {}, {}, {}
    first, second, first_back, second_back = {}, {}, {}, {}

    def order_of(g):
        if not tuned:
            return "all"
        return ("xy", "yx")[g % 2]

    def hop_one(value, g, later):
        if not tuned:
            return scan_generic(value, later == 1)
        return swap(value, "seq", 1 if order_of(g) == "xy" else 2)

    def hop_two(value, brought, g, later):
        if not tuned:
            return brought
        if order_of(g) == "xy":
            return swap(pair(value, brought, f"pair_{later}_{g}"), "seq", 2)
        body = functools.partial(turn_kernel, later)
        (out,) = call(body, [whole(value), whole(brought)], [(value.shape, F32)], f"turn_{later}_{g}")
        return swap(out, "seq", 1)

    def key_state(g):
        outs = [tok(BF16), sq(F32)] * 2
        pair_wide = 2 * wide
        scratch = [
            pltpu.VMEM((rows, pair_wide), BF16),
            pltpu.VMEM((rows, pair_wide), BF16),
            pltpu.VMEM((pair_wide, HEAD), BF16),
            pltpu.SemaphoreType.DMA((3,)),
        ]
        inputs = [in_hbm(key), in_hbm(value), in_hbm(w_key)]
        body = functools.partial(key_kernel, g // 2)
        result = call(body, inputs, outs, f"key_state_{g}", scratch, to_vmem=True, vmem=KEY_VMEM[min(g // 2, 1)])
        feat_k[g], state[g], feat_k[g + 1], state[g + 1] = result
        for k in (g, g + 1):
            first[k] = hop_one(state[k], k, 0)

    def prior_hop(g):
        second[g] = hop_two(state[g], first[g], g, 0)

    def query_attn(g):
        feat_q[g], attn[g] = call(
            query_kernel,
            [cols(query, g), wrows(w_query, g), whole(feat_k[g])],
            [tok(BF16), ((GROUP, rows, rows), BF16)],
            f"query_attn_{g}",
        )

    def numer_state(g):
        numer[g] = call(
            functools.partial(numer_kernel, order_of(g)),
            [whole(first[g]), whole(second[g]), whole(feat_q[g]), whole(attn[g]), cols(value, g), cols(grad, g), cols(gain, g)],
            [sq(F32), tok(BF16), tok(BF16), sq(BF16), sq(BF16), ((GROUP, 8, HEAD), F32)],
            f"numer_{g}",
        )
        first_back[g] = hop_one(numer[g][0], g, 1)

    def later_hop(g):
        second_back[g] = hop_two(numer[g][0], first_back[g], g, 1)

    def query_grad(g):
        _, low, rest, ph, pl_, gains = numer[g]
        mixed[g], back_q[g], sum_q[g] = call(
            query_grad_kernel,
            [whole(x) for x in (low, rest, ph, pl_, feat_k[g])]
            + [cols(query, g), cols(value, g), wrows(w_query, g), whole(gains)],
            [((GROUP, rows, rows), BF16), tok(BF16), ((GROUP, HEAD + 8, HEAD), F32)],
            f"query_grad_{g}",
        )

    def key_grad(g):
        pre_k[g], late_h[g], late_l[g], sum_k[g] = call(
            functools.partial(key_grad_kernel, order_of(g)),
            [whole(first_back[g]), whole(second_back[g]), whole(mixed[g]), whole(feat_q[g])]
            + [cols(key, g), cols(value, g), wrows(w_key, g)],
            [tok(BF16), sq(BF16), sq(BF16), sq(F32)],
            f"key_grad_{g}",
        )

    def value_grad(g):
        back_k[g], back_v[g] = call(
            value_grad_kernel,
            [whole(x) for x in (attn[g], numer[g][1], feat_k[g], late_h[g], late_l[g], pre_k[g])] + [wrows(w_key, g)],
            [tok(BF16), tok(BF16)],
            f"value_grad_{g}",
        )

    hops = {}

    def core_hop(b):
        parts = sum_q if b > 1 else sum_k
        inputs = [whole(parts[2 * (b % 2)]), whole(parts[2 * (b % 2) + 1])]
        shape = (2,) + parts[0].shape[1:]
        both = ((2,) + shape, F32)
        if b == 2:
            kept, sent = call(core_kernel, inputs, [both, both], "core_2")
            hops[b] = (kept, swap(sent, "dp", 1))
        elif b == 3:
            kept, sent, total = call(core_kernel, inputs + [whole(x) for x in hops[2]], [both] * 3, "core_3")
            hops[2] = (total, kept, swap(sent, "dp", 1))
        else:
            kept, *sent = call(core_kernel, inputs, [both, (shape, F32), (shape, F32)], f"core_{b}")
            hops[b] = (kept,) + tuple(swap(x, "dp", 1) for x in sent)

    def far_hop(_):
        kept, sent = call(far_kernel, [whole(x) for x in hops[2]], [(hops[2][0].shape, F32)] * 2, "far")
        hops[2] = (kept, swap(sent, "dp", 4))

    def near_hop(_):
        shape = hops[2][0].shape[1:]
        outs = [(shape, F32), (shape[1:], F32), (shape[1:], F32)]
        kept, *sent = call(near_kernel, [whole(x) for x in hops[2]], outs, "near")
        hops[2] = (kept,) + tuple(swap(x, "dp", 2) for x in sent)

    def z_hop(b):
        inputs = hops[0] + hops[1]
        own, *sent = call(spread_kernel, [whole(x) for x in inputs], [(inputs[1].shape, F32)] * 4, "spread")
        hops[0] = (own,) + tuple(swap(x, "dp", 2 * bits) for bits, x in enumerate(sent, 1))

    totals = {}

    def square(part):
        return (part,) + tuple(swap(part, "seq", bits) for bits in (1, 2, 3))

    def query_first(_):
        parts = call(halves_kernel, [whole(x) for x in hops[2]], [(hops[2][1].shape, F32)] * 2, "query_sum")
        totals["query"] = [(x, swap(x, "seq", bit)) for bit, x in enumerate(parts, 1)]

    def query_second(_):
        parts = call(
            both_pairs_kernel, [whole(x) for x in sum(totals["query"], ())], [(totals["query"][0][0].shape, F32)] * 2, "query_turn"
        )
        totals["query"] = [(x, swap(x, "seq", 2 - bit)) for bit, x in enumerate(parts)]

    def key_square(_):
        (part,) = call(gather_kernel, [whole(x) for x in hops[0]], [(hops[0][0].shape, F32)], "key_sum")
        totals["key"] = square(part)

    rows_out = ((2 * HEAD, HEAD), F32)

    def key_total(_):
        (totals["k"],) = call(key_total_kernel, [whole(x) for x in totals["key"]], [rows_out], "key_total")

    def query_total(_):
        totals["q"], totals["gain"] = call(
            query_total_kernel, [whole(x) for x in sum(totals["query"], ())], [rows_out, ((2, HEAD), F32)], "query_total"
        )

    def listed(by_group):
        return [by_group[g] for g in range(groups)]

    laid = {}

    def lay(k):
        parts = (back_q, back_k, back_v)[k]
        (laid[k],) = call(
            functools.partial(lay_kernel, groups),
            [whole(x) for x in listed(parts)],
            [((rows, width), BF16)],
            f"lay_{k}",
            [pltpu.VMEM((rows, width), BF16), pltpu.SemaphoreType.DMA(())],
            True,
        )

    if tuned:
        steps = (
            "K0K2Q0Q1p1p0Q2Q3p3p2N0N1G0G1N2N3a2G2G3",
            "l0l1a3l2l3B2H0H1a0V0V1H2H3a1V2V3Z0c2L0L1E0C0F0L2T0U0",
        )
        steps = "".join(steps)
    else:
        steps = "".join(f"K{g}" for g in range(0, groups, 2))
        steps += "".join(f"{kind}{g}" for kind in "pQNlGHV" for g in range(groups)) + "L0L1L2"
    does = {
        "K": key_state,
        "p": prior_hop,
        "Q": query_attn,
        "N": numer_state,
        "l": later_hop,
        "G": query_grad,
        "H": key_grad,
        "V": value_grad,
        "L": lay,
        "a": core_hop,
        "B": far_hop,
        "c": near_hop,
        "Z": z_hop,
        "E": query_first,
        "F": query_second,
        "C": key_square,
        "T": key_total,
        "U": query_total,
    }
    for k in range(0, len(steps), 2):
        does[steps[k]](int(steps[k + 1]))
    if tuned:
        total_q, total_k, total_gain = totals["q"], totals["k"], totals["gain"].reshape(2 * HEAD)
    else:

        def in_order(parts):
            return jnp.concatenate(listed(parts), axis=0)

        both = in_order(sum_q)
        owned = (
            lax.psum_scatter(both[:, :HEAD].reshape(width, HEAD), "dp", scatter_dimension=0, tiled=True),
            lax.psum_scatter(in_order(sum_k).reshape(width, HEAD), "dp", scatter_dimension=0, tiled=True),
            lax.psum_scatter(both[:, HEAD].reshape(width), "dp", scatter_dimension=0, tiled=True),
        )
        total_q, total_k, total_gain = lax.psum(owned, "seq")
    shape = query_in.shape
    return (
        laid[0].reshape(shape),
        laid[1].reshape(shape),
        laid[2].reshape(shape),
        total_q,
        total_k,
        total_gain,
    )


def solution(mesh):
    split = P("dp", "seq", None)
    return jax.shard_map(
        per_device,
        mesh=mesh,
        in_specs=(split, split, split, split, P(), P(), P()),
        out_specs=(split, split, split, P("dp", None), P("dp", None), P("dp")),
        check_vma=False,
    )
```

```python
import functools

import jax
import jax.numpy as jnp
from jax import lax
from jax.experimental import pallas as pl
from jax.experimental.pallas import tpu as pltpu
from jax.sharding import PartitionSpec as P

HEAD = 128
GROUP = 4
KEY_VMEM = (64 * 1024 - 4000, 64 * 1024 - 10000)
NORM_EPS = 1e-05
F32 = jnp.float32
BF16 = jnp.bfloat16


def dot(a, b, ca=1, cb=0):
    return lax.dot_general(a, b, (((ca,), (cb,)), ((), ())), preferred_element_type=F32)


def feature(pre):
    return jnp.where(pre > 0.0, pre + 1.0, jnp.exp(jnp.minimum(pre, 0.0)))


def split_low(value):
    high = value.astype(BF16)
    return high, (value - high.astype(F32)).astype(BF16)


def tril(rows):
    return lax.broadcasted_iota(jnp.int32, (rows, rows), 0) >= lax.broadcasted_iota(
        jnp.int32, (rows, rows), 1
    )


def columns(i):
    return slice(i * HEAD, (i + 1) * HEAD)


def place_in_square():
    mine = lax.axis_index("seq")
    return lax.rem(mine, 2), lax.div(mine, 2)


def summed(order, later, first, second):
    if order == "all":
        return [first[i] for i in range(GROUP)]
    at_x, at_y = place_in_square()
    if order == "xy":
        keep_first, keep_second = at_x != later, at_y != later
        return [
            jnp.where(keep_first, first[i], 0.0) + jnp.where(keep_second, second[i], 0.0) for i in range(GROUP)
        ]
    keep_first = at_y != later
    return [jnp.where(keep_first, first[i], 0.0) + second[i] for i in range(GROUP)]


def turn_kernel(later, own, first, out):
    at_x, at_y = place_in_square()
    out[...] = jnp.where(at_y != later, first[...], 0.0) + jnp.where(at_x == later, own[...], 0.0)


def bit_clear(bit):
    return lax.rem(lax.div(lax.axis_index("dp"), bit), 2) == 0


def key_features(key, w_key):
    return [feature(dot(key[:, c], w_key[c, :])).astype(BF16) for c in map(columns, range(2 * GROUP))]


def key_states(low, value, *outs):
    states = [dot(f, value[:, columns(i)], 0, 0) for i, f in enumerate(low)]
    for g in range(2):
        for i in range(GROUP):
            outs[2 * g][i] = low[g * GROUP + i]
            outs[2 * g + 1][i] = states[g * GROUP + i]


def key_kernel(block, key, value, w_key, *refs):
    outs, (key_buf, value_buf, w_buf, sems) = refs[:4], refs[4:]
    span = pl.ds(block * key_buf.shape[1], key_buf.shape[1])
    copies = [
        pltpu.make_async_copy(key.at[:, span], key_buf, sems.at[0]),
        pltpu.make_async_copy(w_key.at[span, :], w_buf, sems.at[1]),
        pltpu.make_async_copy(value.at[:, span], value_buf, sems.at[2]),
    ]
    for copy in copies:
        copy.start()
    copies[0].wait()
    copies[1].wait()
    low = key_features(key_buf, w_buf)
    copies[2].wait()
    key_states(low, value_buf, *outs)


def query_kernel(query, w_query, feat_key, feat_query, attn):
    causal = tril(query.shape[0])
    at = [columns(i) for i in range(GROUP)]
    low = [feature(dot(query[:, c], w_query[c, :])).astype(BF16) for c in at]
    scores = [dot(low[i], feat_key[i], 1, 1) for i in range(GROUP)]
    for i in range(GROUP):
        feat_query[i] = low[i]
        attn[i] = jnp.where(causal, scores[i], 0.0).astype(BF16)


def numer_kernel(order, first, second, feat_query, attn, value, grad, gain, adjoint, low_out, rest_out, ph_out, pl_out, gain_out):
    every = range(GROUP)
    at = [columns(i) for i in every]
    inner = [dot(attn[i], value[:, at[i]]) for i in every]
    prior = summed(order, 0, first, second)
    parts = [split_low(p) for p in prior]
    feat = [feat_query[i] for i in every]
    numer = [inner[i] + dot(feat[i], parts[i][0]) + dot(feat[i], parts[i][1]) for i in every]
    inv = [lax.rsqrt(jnp.mean(n * n, axis=-1, keepdims=True) + NORM_EPS) for n in numer]
    normed = [n * r for n, r in zip(numer, inv)]
    grad_f = [grad[:, c].astype(F32) for c in at]
    scaled = [x * gain[:, c] for x, c in zip(grad_f, at)]
    means = [jnp.mean(x * n, axis=-1, keepdims=True) for x, n in zip(scaled, normed)]
    grads = [split_low(inv[i] * (scaled[i] - normed[i] * means[i])) for i in every]
    states = [dot(feat[i], grads[i][0], 0, 0) for i in every]
    for i in every:
        adjoint[i] = states[i]
        low_out[i], rest_out[i] = grads[i]
        ph_out[i], pl_out[i] = parts[i]
        gain_out[i] = jnp.broadcast_to(jnp.sum(normed[i] * grad_f[i], axis=0, keepdims=True), (8, HEAD))


def query_grad_kernel(numer_low, rest, high, low, feat_key, query, value, w_query, gain, mixed_out, grad_out, weight):
    causal = tril(query.shape[0])
    every = range(GROUP)
    at = [columns(i) for i in every]
    grad_low = [numer_low[i] for i in every]
    slope = [jnp.minimum(feature(dot(query[:, c], w_query[c, :])), 1.0) for c in at]
    raw = [dot(grad_low[i], value[:, at[i]], 1, 1) for i in every]
    mixed = [jnp.where(causal, x, 0.0).astype(BF16) for x in raw]
    grad_fq = [
        dot(mixed[i], feat_key[i])
        + dot(grad_low[i], high[i], 1, 1)
        + dot(grad_low[i], low[i], 1, 1)
        + dot(rest[i], high[i], 1, 1)
        for i in every
    ]
    pre = [(grad_fq[i] * slope[i]).astype(BF16) for i in every]
    sums = [dot(query[:, at[i]], pre[i], 0, 0) for i in every]
    back = [dot(pre[i], w_query[at[i], :], 1, 1) for i in every]
    for i in every:
        mixed_out[i] = mixed[i]
        grad_out[i] = back[i].astype(BF16)
        weight[i, :HEAD, :] = sums[i]
        weight[i, HEAD:, :] = gain[i]


def key_grad_kernel(order, first, second, mixed, feat_query, key, value, w_key, pre_out, lh_out, ll_out, weight):
    every = range(GROUP)
    at = [columns(i) for i in every]
    slope = [jnp.minimum(feature(dot(key[:, c], w_key[c, :])), 1.0) for c in at]
    later = summed(order, 1, first, second)
    parts = [split_low(x) for x in later]
    val = [value[:, c] for c in at]
    grad_fk = [
        dot(mixed[i], feat_query[i], 0, 0) + dot(val[i], parts[i][0], 1, 1) + dot(val[i], parts[i][1], 1, 1)
        for i in every
    ]
    pre = [(grad_fk[i] * slope[i]).astype(BF16) for i in every]
    sums = [dot(key[:, at[i]], pre[i], 0, 0) for i in every]
    for i in every:
        weight[i] = sums[i]
        pre_out[i] = pre[i]
        lh_out[i], ll_out[i] = parts[i]


def value_grad_kernel(attn, numer_low, feat_key, high, low, pre, w_key, key_out, value_out):
    every = range(GROUP)
    feat = [feat_key[i] for i in every]
    grads = [
        dot(attn[i], numer_low[i], 0, 0) + dot(feat[i], high[i]) + dot(feat[i], low[i]) for i in every
    ]
    back = [dot(pre[i], w_key[columns(i), :], 1, 1) for i in every]
    for i in every:
        value_out[i] = grads[i].astype(BF16)
        key_out[i] = back[i].astype(BF16)


def lay_kernel(groups, *refs):
    out, laid, sem = refs[groups:]
    for g in range(groups):
        for i in range(GROUP):
            laid[:, place(g, i)] = refs[g][i]
    copy = pltpu.make_async_copy(laid, out, sem)
    copy.start()
    copy.wait()


def pair_kernel(one, two, out):
    out[...] = one[...] + two[...]


def core_kernel(low, high, *refs):
    if len(refs) == 5:
        one, two, kept, *sent, total = refs
        total[...] = one[...] + two[...]
    else:
        kept, *sent = refs
    first = bit_clear(1)
    for m, part in enumerate((low, high)):
        for b in range(2):
            one, two = part[b], part[2 + b]
            kept[m, b] = jnp.where(first, one, two)
            out = jnp.where(first, two, one)
            if len(sent) == 2:
                sent[m][b] = out
            else:
                sent[0][m, b] = out


def far_kernel(low, own, theirs, kept, sent):
    first = bit_clear(4)
    high = own[...] + theirs[...]
    kept[...] = jnp.where(first, low[...], high)
    sent[...] = jnp.where(first, high, low[...])


def near_kernel(mine, theirs, kept, *sent):
    first = bit_clear(2)
    one, two = mine[0] + theirs[0], mine[1] + theirs[1]
    kept[...] = jnp.where(first, one, two)
    out = jnp.where(first, two, one)
    for b in range(2):
        sent[b][...] = out[b]


def spread_kernel(*refs):
    parts, outs = refs[:6], refs[6:]
    near, far = bit_clear(2), bit_clear(4)
    for m in range(2):
        low = parts[0][m] + parts[1 + m][...]
        high = parts[3][m] + parts[4 + m][...]
        here, there = jnp.where(far, low, high), jnp.where(far, high, low)
        same = near if m == 0 else jnp.logical_not(near)

        @pl.when(same)
        def _():
            outs[0][...] = here
            outs[2][...] = there

        @pl.when(jnp.logical_not(same))
        def _():
            outs[1][...] = here
            outs[3][...] = there


def gather_kernel(own, near, far, both, out):
    out[...] = (own[...] + near[...]) + (far[...] + both[...])


def half_kernel(b, own, other, out):
    out[...] = own[b] + other[...]


def key_total_kernel(key, key_x, key_y, key_d, out):
    total = (key[...] + key_x[...]) + (key_y[...] + key_d[...])
    for b in range(2):
        out[b * HEAD : (b + 1) * HEAD, :] = total[b]


def query_total_kernel(even, even_other, odd, odd_other, out, out_gain):
    for b, (one, two) in enumerate(((even, even_other), (odd, odd_other))):
        total = one[...] + two[...]
        out[b * HEAD : (b + 1) * HEAD, :] = total[:HEAD, :]
        out_gain[b : b + 1, :] = total[HEAD : HEAD + 1, :]


def place(g, i):
    at = (g * GROUP + i) * HEAD
    return slice(at, at + HEAD)


class Order:
    def __init__(self):
        self.last = None

    def __call__(self, body, ins, outs, name, scratch=(), to_hbm=False, to_vmem=False, chain=True, vmem=12 * 1024):
        at = len(ins)
        after = chain and self.last is not None
        if after:
            ins = ins + [(self.last, pl.BlockSpec(memory_space=pl.ANY))]
        inputs, results = len(ins), len(outs)

        def ordered(*refs):
            body(*refs[:at], *refs[inputs : inputs + results], *refs[inputs + results + chain :])
            if chain:
                token = refs[inputs + results]
                token[...] = jnp.zeros_like(token)

        out_specs = [
            pl.BlockSpec(memory_space=pltpu.HBM) if to_hbm else pl.BlockSpec(shape, lambda _, n=len(shape): (0,) * n)
            for shape, _ in outs
        ]
        out_shape = [jax.ShapeDtypeStruct(shape, kind) for shape, kind in outs]
        if to_vmem:
            out_specs = [pl.BlockSpec(memory_space=pltpu.VMEM) for _ in outs]
            out_shape = [pltpu.VMEM(shape, kind) for shape, kind in outs]
        if chain and to_vmem:
            out_specs.append(pl.BlockSpec(memory_space=pltpu.VMEM))
            out_shape.append(pltpu.VMEM((8, HEAD), F32))
        elif chain:
            out_specs.append(pl.BlockSpec((8, HEAD), lambda _: (0, 0)))
            out_shape.append(jax.ShapeDtypeStruct((8, HEAD), F32))
        result = pl.pallas_call(
            ordered,
            grid=(1,),
            in_specs=[spec for _, spec in ins],
            out_specs=out_specs,
            out_shape=out_shape,
            scratch_shapes=list(scratch),
            compiler_params=pltpu.CompilerParams(vmem_limit_bytes=vmem * 1024),
            cost_estimate=pl.CostEstimate(flops=200000000, bytes_accessed=0, transcendentals=0),
            name=name,
        )(*[x for x, _ in ins])
        if chain:
            self.last = result[-1]
            return result[:-1]
        return result


def whole(x):
    return (x, pl.BlockSpec(x.shape, lambda _, n=x.ndim: (0,) * n))


def in_hbm(x):
    return (x, pl.BlockSpec(memory_space=pltpu.HBM))


def scan_generic(value, reverse):
    peers, mine = lax.axis_size("seq"), lax.axis_index("seq")
    everything = lax.all_gather(value, "seq")

    def turn(k, before):
        reached = k > mine if reverse else k < mine
        return before + jnp.where(reached, everything[k], 0.0)

    return lax.fori_loop(0, peers, turn, jnp.zeros_like(value))


def swap(value, axis, bit):
    return lax.ppermute(value, axis, [(i, i ^ bit) for i in range(lax.axis_size(axis))])


def per_device(query_in, key_in, value_in, grad_out, w_query, w_key, norm_gain):
    _, rows, width = query_in.shape
    heads = width // HEAD
    groups = heads // GROUP
    tuned = lax.axis_size("seq") == 4 and lax.axis_size("dp") == 8 and heads == 16
    query, key, value, grad = (x.reshape(rows, width) for x in (query_in, key_in, value_in, grad_out))
    gain = norm_gain.reshape(1, width)
    wide = GROUP * HEAD

    def cols(x, g):
        return (x, pl.BlockSpec((x.shape[0], wide), lambda _: (0, g)))

    def wrows(x, g):
        return (x, pl.BlockSpec((wide, HEAD), lambda _: (g, 0)))

    def tok(kind):
        return ((GROUP, rows, HEAD), kind)

    def sq(kind):
        return ((GROUP, HEAD, HEAD), kind)

    call = Order()

    def pair(one, two, name):
        (out,) = call(pair_kernel, [whole(one), whole(two)], [(one.shape, F32)], name)
        return out

    feat_k, state, feat_q, attn = {}, {}, {}, {}
    numer, mixed, back_q, sum_q = {}, {}, {}, {}
    pre_k, late_h, late_l, sum_k, back_k, back_v = {}, {}, {}, {}, {}, {}
    first, second, first_back, second_back = {}, {}, {}, {}

    def order_of(g):
        if not tuned:
            return "all"
        return ("xy", "yx")[g % 2]

    def hop_one(value, g, later):
        if not tuned:
            return scan_generic(value, later == 1)
        return swap(value, "seq", 1 if order_of(g) == "xy" else 2)

    def hop_two(value, brought, g, later):
        if not tuned:
            return brought
        if order_of(g) == "xy":
            return swap(pair(value, brought, f"pair_{later}_{g}"), "seq", 2)
        body = functools.partial(turn_kernel, later)
        (out,) = call(body, [whole(value), whole(brought)], [(value.shape, F32)], f"turn_{later}_{g}")
        return swap(out, "seq", 1)

    def key_state(g):
        outs = [tok(BF16), sq(F32)] * 2
        pair_wide = 2 * wide
        scratch = [
            pltpu.VMEM((rows, pair_wide), BF16),
            pltpu.VMEM((rows, pair_wide), BF16),
            pltpu.VMEM((pair_wide, HEAD), BF16),
            pltpu.SemaphoreType.DMA((3,)),
        ]
        inputs = [in_hbm(key), in_hbm(value), in_hbm(w_key)]
        body = functools.partial(key_kernel, g // 2)
        result = call(body, inputs, outs, f"key_state_{g}", scratch, to_vmem=True, vmem=KEY_VMEM[min(g // 2, 1)])
        feat_k[g], state[g], feat_k[g + 1], state[g + 1] = result
        for k in (g, g + 1):
            first[k] = hop_one(state[k], k, 0)

    def prior_hop(g):
        second[g] = hop_two(state[g], first[g], g, 0)

    def query_attn(g):
        feat_q[g], attn[g] = call(
            query_kernel,
            [cols(query, g), wrows(w_query, g), whole(feat_k[g])],
            [tok(BF16), ((GROUP, rows, rows), BF16)],
            f"query_attn_{g}",
        )

    def numer_state(g):
        numer[g] = call(
            functools.partial(numer_kernel, order_of(g)),
            [whole(first[g]), whole(second[g]), whole(feat_q[g]), whole(attn[g]), cols(value, g), cols(grad, g), cols(gain, g)],
            [sq(F32), tok(BF16), tok(BF16), sq(BF16), sq(BF16), ((GROUP, 8, HEAD), F32)],
            f"numer_{g}",
        )
        first_back[g] = hop_one(numer[g][0], g, 1)

    def later_hop(g):
        second_back[g] = hop_two(numer[g][0], first_back[g], g, 1)

    def query_grad(g):
        _, low, rest, ph, pl_, gains = numer[g]
        mixed[g], back_q[g], sum_q[g] = call(
            query_grad_kernel,
            [whole(x) for x in (low, rest, ph, pl_, feat_k[g])]
            + [cols(query, g), cols(value, g), wrows(w_query, g), whole(gains)],
            [((GROUP, rows, rows), BF16), tok(BF16), ((GROUP, HEAD + 8, HEAD), F32)],
            f"query_grad_{g}",
        )

    def key_grad(g):
        pre_k[g], late_h[g], late_l[g], sum_k[g] = call(
            functools.partial(key_grad_kernel, order_of(g)),
            [whole(first_back[g]), whole(second_back[g]), whole(mixed[g]), whole(feat_q[g])]
            + [cols(key, g), cols(value, g), wrows(w_key, g)],
            [tok(BF16), sq(BF16), sq(BF16), sq(F32)],
            f"key_grad_{g}",
        )

    def value_grad(g):
        back_k[g], back_v[g] = call(
            value_grad_kernel,
            [whole(x) for x in (attn[g], numer[g][1], feat_k[g], late_h[g], late_l[g], pre_k[g])] + [wrows(w_key, g)],
            [tok(BF16), tok(BF16)],
            f"value_grad_{g}",
        )

    hops = {}

    def core_hop(b):
        parts = sum_q if b > 1 else sum_k
        inputs = [whole(parts[2 * (b % 2)]), whole(parts[2 * (b % 2) + 1])]
        shape = (2,) + parts[0].shape[1:]
        both = ((2,) + shape, F32)
        if b == 2:
            kept, sent = call(core_kernel, inputs, [both, both], "core_2")
            hops[b] = (kept, swap(sent, "dp", 1))
        elif b == 3:
            kept, sent, total = call(core_kernel, inputs + [whole(x) for x in hops[2]], [both] * 3, "core_3")
            hops[2] = (total, kept, swap(sent, "dp", 1))
        else:
            kept, *sent = call(core_kernel, inputs, [both, (shape, F32), (shape, F32)], f"core_{b}")
            hops[b] = (kept,) + tuple(swap(x, "dp", 1) for x in sent)

    def far_hop(_):
        kept, sent = call(far_kernel, [whole(x) for x in hops[2]], [(hops[2][0].shape, F32)] * 2, "far")
        hops[2] = (kept, swap(sent, "dp", 4))

    def near_hop(_):
        shape = hops[2][0].shape[1:]
        outs = [(shape, F32), (shape[1:], F32), (shape[1:], F32)]
        kept, *sent = call(near_kernel, [whole(x) for x in hops[2]], outs, "near")
        hops[2] = (kept,) + tuple(swap(x, "dp", 2) for x in sent)

    def z_hop(b):
        inputs = hops[0] + hops[1]
        own, *sent = call(spread_kernel, [whole(x) for x in inputs], [(inputs[1].shape, F32)] * 4, "spread")
        hops[0] = (own,) + tuple(swap(x, "dp", 2 * bits) for bits, x in enumerate(sent, 1))

    totals = {}

    def square(part):
        return (part,) + tuple(swap(part, "seq", bits) for bits in (1, 2, 3))

    def query_first(b):
        own, other = hops[2][0], hops[2][1 + b]
        (part,) = call(functools.partial(half_kernel, b), [whole(own), whole(other)], [(other.shape, F32)], f"query_sum_{b}")
        totals["query", b] = (part, swap(part, "seq", 1 + b))

    def query_second(b):
        part = pair(*totals["query", b], f"query_turn_{b}")
        totals["query", b] = (part, swap(part, "seq", 2 - b))

    def key_square(_):
        (part,) = call(gather_kernel, [whole(x) for x in hops[0]], [(hops[0][0].shape, F32)], "key_sum")
        totals["key"] = square(part)

    rows_out = ((2 * HEAD, HEAD), F32)

    def key_total(_):
        (totals["k"],) = call(key_total_kernel, [whole(x) for x in totals["key"]], [rows_out], "key_total")

    def query_total(_):
        totals["q"], totals["gain"] = call(
            query_total_kernel, [whole(x) for x in totals["query", 0] + totals["query", 1]], [rows_out, ((2, HEAD), F32)], "query_total"
        )

    def listed(by_group):
        return [by_group[g] for g in range(groups)]

    laid = {}

    def lay(k):
        parts = (back_q, back_k, back_v)[k]
        (laid[k],) = call(
            functools.partial(lay_kernel, groups),
            [whole(x) for x in listed(parts)],
            [((rows, width), BF16)],
            f"lay_{k}",
            [pltpu.VMEM((rows, width), BF16), pltpu.SemaphoreType.DMA(())],
            True,
        )

    if tuned:
        steps = (
            "K0K2Q0Q1p1p0Q2Q3p3p2N0N1G0G1N2N3a2G2G3",
            "l0l1a3l2l3B2H0H1a0V0V1H2H3a1V2V3Z0c2L0L1E0E1C0F0F1L2T0U0",
        )
        steps = "".join(steps)
    else:
        steps = "".join(f"K{g}" for g in range(0, groups, 2))
        steps += "".join(f"{kind}{g}" for kind in "pQNlGHV" for g in range(groups)) + "L0L1L2"
    does = {
        "K": key_state,
        "p": prior_hop,
        "Q": query_attn,
        "N": numer_state,
        "l": later_hop,
        "G": query_grad,
        "H": key_grad,
        "V": value_grad,
        "L": lay,
        "a": core_hop,
        "B": far_hop,
        "c": near_hop,
        "Z": z_hop,
        "E": query_first,
        "F": query_second,
        "C": key_square,
        "T": key_total,
        "U": query_total,
    }
    for k in range(0, len(steps), 2):
        does[steps[k]](int(steps[k + 1]))
    if tuned:
        total_q, total_k, total_gain = totals["q"], totals["k"], totals["gain"].reshape(2 * HEAD)
    else:

        def in_order(parts):
            return jnp.concatenate(listed(parts), axis=0)

        both = in_order(sum_q)
        owned = (
            lax.psum_scatter(both[:, :HEAD].reshape(width, HEAD), "dp", scatter_dimension=0, tiled=True),
            lax.psum_scatter(in_order(sum_k).reshape(width, HEAD), "dp", scatter_dimension=0, tiled=True),
            lax.psum_scatter(both[:, HEAD].reshape(width), "dp", scatter_dimension=0, tiled=True),
        )
        total_q, total_k, total_gain = lax.psum(owned, "seq")
    shape = query_in.shape
    return (
        laid[0].reshape(shape),
        laid[1].reshape(shape),
        laid[2].reshape(shape),
        total_q,
        total_k,
        total_gain,
    )


def solution(mesh):
    split = P("dp", "seq", None)
    return jax.shard_map(
        per_device,
        mesh=mesh,
        in_specs=(split, split, split, split, P(), P(), P()),
        out_specs=(split, split, split, P("dp", None), P("dp", None), P("dp")),
        check_vma=False,
    )
```

```python
import functools

import jax
import jax.numpy as jnp
from jax import lax
from jax.experimental import pallas as pl
from jax.experimental.pallas import tpu as pltpu
from jax.sharding import PartitionSpec as P

HEAD = 128
GROUP = 4
KEY_VMEM = (64 * 1024 - 4000, 64 * 1024 - 10000)
NORM_EPS = 1e-05
F32 = jnp.float32
BF16 = jnp.bfloat16


def dot(a, b, ca=1, cb=0):
    return lax.dot_general(a, b, (((ca,), (cb,)), ((), ())), preferred_element_type=F32)


def feature(pre):
    return jnp.where(pre > 0.0, pre + 1.0, jnp.exp(jnp.minimum(pre, 0.0)))


def split_low(value):
    high = value.astype(BF16)
    return high, (value - high.astype(F32)).astype(BF16)


def tril(rows):
    return lax.broadcasted_iota(jnp.int32, (rows, rows), 0) >= lax.broadcasted_iota(
        jnp.int32, (rows, rows), 1
    )


def columns(i):
    return slice(i * HEAD, (i + 1) * HEAD)


def place_in_square():
    mine = lax.axis_index("seq")
    return lax.rem(mine, 2), lax.div(mine, 2)


def summed(order, later, first, second):
    if order == "all":
        return [first[i] for i in range(GROUP)]
    at_x, at_y = place_in_square()
    if order == "xy":
        keep_first, keep_second = at_x != later, at_y != later
        return [
            jnp.where(keep_first, first[i], 0.0) + jnp.where(keep_second, second[i], 0.0) for i in range(GROUP)
        ]
    keep_first = at_y != later
    return [jnp.where(keep_first, first[i], 0.0) + second[i] for i in range(GROUP)]


def turn_kernel(later, own, first, out):
    at_x, at_y = place_in_square()
    out[...] = jnp.where(at_y != later, first[...], 0.0) + jnp.where(at_x == later, own[...], 0.0)


def bit_clear(bit):
    return lax.rem(lax.div(lax.axis_index("dp"), bit), 2) == 0


def key_features(key, w_key):
    return [feature(dot(key[:, c], w_key[c, :])).astype(BF16) for c in map(columns, range(2 * GROUP))]


def key_states(low, value, *outs):
    states = [dot(f, value[:, columns(i)], 0, 0) for i, f in enumerate(low)]
    for g in range(2):
        for i in range(GROUP):
            outs[2 * g][i] = low[g * GROUP + i]
            outs[2 * g + 1][i] = states[g * GROUP + i]


def key_kernel(block, key, value, w_key, *refs):
    outs, (key_buf, value_buf, w_buf, sems) = refs[:4], refs[4:]
    span = pl.ds(block * key_buf.shape[1], key_buf.shape[1])
    copies = [
        pltpu.make_async_copy(key.at[:, span], key_buf, sems.at[0]),
        pltpu.make_async_copy(w_key.at[span, :], w_buf, sems.at[1]),
        pltpu.make_async_copy(value.at[:, span], value_buf, sems.at[2]),
    ]
    for copy in copies:
        copy.start()
    copies[0].wait()
    copies[1].wait()
    low = key_features(key_buf, w_buf)
    copies[2].wait()
    key_states(low, value_buf, *outs)


def query_kernel(query, w_query, feat_key, feat_query, attn):
    causal = tril(query.shape[0])
    at = [columns(i) for i in range(GROUP)]
    low = [feature(dot(query[:, c], w_query[c, :])).astype(BF16) for c in at]
    scores = [dot(low[i], feat_key[i], 1, 1) for i in range(GROUP)]
    for i in range(GROUP):
        feat_query[i] = low[i]
        attn[i] = jnp.where(causal, scores[i], 0.0).astype(BF16)


def numer_kernel(order, first, second, feat_query, attn, value, grad, gain, adjoint, low_out, rest_out, ph_out, pl_out, gain_out):
    every = range(GROUP)
    at = [columns(i) for i in every]
    inner = [dot(attn[i], value[:, at[i]]) for i in every]
    prior = summed(order, 0, first, second)
    parts = [split_low(p) for p in prior]
    feat = [feat_query[i] for i in every]
    numer = [inner[i] + dot(feat[i], parts[i][0]) + dot(feat[i], parts[i][1]) for i in every]
    inv = [lax.rsqrt(jnp.mean(n * n, axis=-1, keepdims=True) + NORM_EPS) for n in numer]
    normed = [n * r for n, r in zip(numer, inv)]
    grad_f = [grad[:, c].astype(F32) for c in at]
    scaled = [x * gain[:, c] for x, c in zip(grad_f, at)]
    means = [jnp.mean(x * n, axis=-1, keepdims=True) for x, n in zip(scaled, normed)]
    grads = [split_low(inv[i] * (scaled[i] - normed[i] * means[i])) for i in every]
    states = [dot(feat[i], grads[i][0], 0, 0) for i in every]
    for i in every:
        adjoint[i] = states[i]
        low_out[i], rest_out[i] = grads[i]
        ph_out[i], pl_out[i] = parts[i]
        gain_out[i] = jnp.broadcast_to(jnp.sum(normed[i] * grad_f[i], axis=0, keepdims=True), (8, HEAD))


def query_grad_kernel(numer_low, rest, high, low, feat_key, query, value, w_query, gain, mixed_out, grad_out, weight):
    causal = tril(query.shape[0])
    every = range(GROUP)
    at = [columns(i) for i in every]
    grad_low = [numer_low[i] for i in every]
    slope = [jnp.minimum(feature(dot(query[:, c], w_query[c, :])), 1.0) for c in at]
    raw = [dot(grad_low[i], value[:, at[i]], 1, 1) for i in every]
    mixed = [jnp.where(causal, x, 0.0).astype(BF16) for x in raw]
    grad_fq = [
        dot(mixed[i], feat_key[i])
        + dot(grad_low[i], high[i], 1, 1)
        + dot(grad_low[i], low[i], 1, 1)
        + dot(rest[i], high[i], 1, 1)
        for i in every
    ]
    pre = [(grad_fq[i] * slope[i]).astype(BF16) for i in every]
    sums = [dot(query[:, at[i]], pre[i], 0, 0) for i in every]
    back = [dot(pre[i], w_query[at[i], :], 1, 1) for i in every]
    for i in every:
        mixed_out[i] = mixed[i]
        grad_out[i] = back[i].astype(BF16)
        weight[i, :HEAD, :] = sums[i]
        weight[i, HEAD:, :] = gain[i]


def key_base_kernel(mixed, feat_query, key, w_key, base_out, slope_out):
    every = range(GROUP)
    at = [columns(i) for i in every]
    slope = [jnp.minimum(feature(dot(key[:, c], w_key[c, :])), 1.0) for c in at]
    base = [dot(mixed[i], feat_query[i], 0, 0) for i in every]
    for i in every:
        base_out[i] = base[i]
        slope_out[i] = slope[i]


def key_grad_kernel(order, first, second, base, slope, key, value, pre_out, lh_out, ll_out, weight):
    every = range(GROUP)
    at = [columns(i) for i in every]
    parts = [split_low(x) for x in summed(order, 1, first, second)]
    val = [value[:, c] for c in at]
    grad_fk = [base[i] + dot(val[i], parts[i][0], 1, 1) + dot(val[i], parts[i][1], 1, 1) for i in every]
    pre = [(grad_fk[i] * slope[i]).astype(BF16) for i in every]
    sums = [dot(key[:, at[i]], pre[i], 0, 0) for i in every]
    for i in every:
        weight[i] = sums[i]
        pre_out[i] = pre[i]
        lh_out[i], ll_out[i] = parts[i]


def value_grad_kernel(attn, numer_low, feat_key, high, low, pre, w_key, key_out, value_out):
    every = range(GROUP)
    feat = [feat_key[i] for i in every]
    grads = [
        dot(attn[i], numer_low[i], 0, 0) + dot(feat[i], high[i]) + dot(feat[i], low[i]) for i in every
    ]
    back = [dot(pre[i], w_key[columns(i), :], 1, 1) for i in every]
    for i in every:
        value_out[i] = grads[i].astype(BF16)
        key_out[i] = back[i].astype(BF16)


def lay_kernel(groups, *refs):
    out, laid, sem = refs[groups:]
    for g in range(groups):
        for i in range(GROUP):
            laid[:, place(g, i)] = refs[g][i]
    copy = pltpu.make_async_copy(laid, out, sem)
    copy.start()
    copy.wait()


def pair_kernel(one, two, out):
    out[...] = one[...] + two[...]


def core_kernel(low, high, *refs):
    if len(refs) == 5:
        one, two, kept, *sent, total = refs
        total[...] = one[...] + two[...]
    else:
        kept, *sent = refs
    first = bit_clear(1)
    for m, part in enumerate((low, high)):
        for b in range(2):
            one, two = part[b], part[2 + b]
            kept[m, b] = jnp.where(first, one, two)
            out = jnp.where(first, two, one)
            if len(sent) == 2:
                sent[m][b] = out
            else:
                sent[0][m, b] = out


def far_kernel(low, own, theirs, kept, sent):
    first = bit_clear(4)
    high = own[...] + theirs[...]
    kept[...] = jnp.where(first, low[...], high)
    sent[...] = jnp.where(first, high, low[...])


def near_kernel(mine, theirs, kept, *sent):
    first = bit_clear(2)
    one, two = mine[0] + theirs[0], mine[1] + theirs[1]
    kept[...] = jnp.where(first, one, two)
    out = jnp.where(first, two, one)
    for b in range(2):
        sent[b][...] = out[b]


def spread_kernel(*refs):
    parts, outs = refs[:6], refs[6:]
    near, far = bit_clear(2), bit_clear(4)
    for m in range(2):
        low = parts[0][m] + parts[1 + m][...]
        high = parts[3][m] + parts[4 + m][...]
        here, there = jnp.where(far, low, high), jnp.where(far, high, low)
        same = near if m == 0 else jnp.logical_not(near)

        @pl.when(same)
        def _():
            outs[0][...] = here
            outs[2][...] = there

        @pl.when(jnp.logical_not(same))
        def _():
            outs[1][...] = here
            outs[3][...] = there


def gather_kernel(own, near, far, both, out):
    out[...] = (own[...] + near[...]) + (far[...] + both[...])


def half_kernel(b, own, other, out):
    out[...] = own[b] + other[...]


def key_total_kernel(key, key_x, key_y, key_d, out):
    total = (key[...] + key_x[...]) + (key_y[...] + key_d[...])
    for b in range(2):
        out[b * HEAD : (b + 1) * HEAD, :] = total[b]


def query_total_kernel(even, even_other, odd, odd_other, out, out_gain):
    for b, (one, two) in enumerate(((even, even_other), (odd, odd_other))):
        total = one[...] + two[...]
        out[b * HEAD : (b + 1) * HEAD, :] = total[:HEAD, :]
        out_gain[b : b + 1, :] = total[HEAD : HEAD + 1, :]


def place(g, i):
    at = (g * GROUP + i) * HEAD
    return slice(at, at + HEAD)


class Order:
    def __init__(self):
        self.last = None

    def __call__(self, body, ins, outs, name, scratch=(), to_hbm=False, to_vmem=False, chain=True, vmem=12 * 1024):
        at = len(ins)
        after = chain and self.last is not None
        if after:
            ins = ins + [(self.last, pl.BlockSpec(memory_space=pl.ANY))]
        inputs, results = len(ins), len(outs)

        def ordered(*refs):
            body(*refs[:at], *refs[inputs : inputs + results], *refs[inputs + results + chain :])
            if chain:
                token = refs[inputs + results]
                token[...] = jnp.zeros_like(token)

        out_specs = [
            pl.BlockSpec(memory_space=pltpu.HBM) if to_hbm else pl.BlockSpec(shape, lambda _, n=len(shape): (0,) * n)
            for shape, _ in outs
        ]
        out_shape = [jax.ShapeDtypeStruct(shape, kind) for shape, kind in outs]
        if to_vmem:
            out_specs = [pl.BlockSpec(memory_space=pltpu.VMEM) for _ in outs]
            out_shape = [pltpu.VMEM(shape, kind) for shape, kind in outs]
        if chain and to_vmem:
            out_specs.append(pl.BlockSpec(memory_space=pltpu.VMEM))
            out_shape.append(pltpu.VMEM((8, HEAD), F32))
        elif chain:
            out_specs.append(pl.BlockSpec((8, HEAD), lambda _: (0, 0)))
            out_shape.append(jax.ShapeDtypeStruct((8, HEAD), F32))
        result = pl.pallas_call(
            ordered,
            grid=(1,),
            in_specs=[spec for _, spec in ins],
            out_specs=out_specs,
            out_shape=out_shape,
            scratch_shapes=list(scratch),
            compiler_params=pltpu.CompilerParams(vmem_limit_bytes=vmem * 1024),
            cost_estimate=pl.CostEstimate(flops=200000000, bytes_accessed=0, transcendentals=0),
            name=name,
        )(*[x for x, _ in ins])
        if chain:
            self.last = result[-1]
            return result[:-1]
        return result


def whole(x):
    return (x, pl.BlockSpec(x.shape, lambda _, n=x.ndim: (0,) * n))


def in_hbm(x):
    return (x, pl.BlockSpec(memory_space=pltpu.HBM))


def scan_generic(value, reverse):
    peers, mine = lax.axis_size("seq"), lax.axis_index("seq")
    everything = lax.all_gather(value, "seq")

    def turn(k, before):
        reached = k > mine if reverse else k < mine
        return before + jnp.where(reached, everything[k], 0.0)

    return lax.fori_loop(0, peers, turn, jnp.zeros_like(value))


def swap(value, axis, bit):
    return lax.ppermute(value, axis, [(i, i ^ bit) for i in range(lax.axis_size(axis))])


def per_device(query_in, key_in, value_in, grad_out, w_query, w_key, norm_gain):
    _, rows, width = query_in.shape
    heads = width // HEAD
    groups = heads // GROUP
    tuned = lax.axis_size("seq") == 4 and lax.axis_size("dp") == 8 and heads == 16
    query, key, value, grad = (x.reshape(rows, width) for x in (query_in, key_in, value_in, grad_out))
    gain = norm_gain.reshape(1, width)
    wide = GROUP * HEAD

    def cols(x, g):
        return (x, pl.BlockSpec((x.shape[0], wide), lambda _: (0, g)))

    def wrows(x, g):
        return (x, pl.BlockSpec((wide, HEAD), lambda _: (g, 0)))

    def tok(kind):
        return ((GROUP, rows, HEAD), kind)

    def sq(kind):
        return ((GROUP, HEAD, HEAD), kind)

    call = Order()

    def pair(one, two, name):
        (out,) = call(pair_kernel, [whole(one), whole(two)], [(one.shape, F32)], name)
        return out

    feat_k, state, feat_q, attn = {}, {}, {}, {}
    numer, mixed, back_q, sum_q = {}, {}, {}, {}
    pre_k, late_h, late_l, sum_k, back_k, back_v = {}, {}, {}, {}, {}, {}
    first, second, first_back, second_back = {}, {}, {}, {}

    def order_of(g):
        if not tuned:
            return "all"
        return ("xy", "yx")[g % 2]

    def hop_one(value, g, later):
        if not tuned:
            return scan_generic(value, later == 1)
        return swap(value, "seq", 1 if order_of(g) == "xy" else 2)

    def hop_two(value, brought, g, later):
        if not tuned:
            return brought
        if order_of(g) == "xy":
            return swap(pair(value, brought, f"pair_{later}_{g}"), "seq", 2)
        body = functools.partial(turn_kernel, later)
        (out,) = call(body, [whole(value), whole(brought)], [(value.shape, F32)], f"turn_{later}_{g}")
        return swap(out, "seq", 1)

    def key_state(g):
        outs = [tok(BF16), sq(F32)] * 2
        pair_wide = 2 * wide
        scratch = [
            pltpu.VMEM((rows, pair_wide), BF16),
            pltpu.VMEM((rows, pair_wide), BF16),
            pltpu.VMEM((pair_wide, HEAD), BF16),
            pltpu.SemaphoreType.DMA((3,)),
        ]
        inputs = [in_hbm(key), in_hbm(value), in_hbm(w_key)]
        body = functools.partial(key_kernel, g // 2)
        result = call(body, inputs, outs, f"key_state_{g}", scratch, to_vmem=True, vmem=KEY_VMEM[min(g // 2, 1)])
        feat_k[g], state[g], feat_k[g + 1], state[g + 1] = result
        for k in (g, g + 1):
            first[k] = hop_one(state[k], k, 0)

    def prior_hop(g):
        second[g] = hop_two(state[g], first[g], g, 0)

    def query_attn(g):
        feat_q[g], attn[g] = call(
            query_kernel,
            [cols(query, g), wrows(w_query, g), whole(feat_k[g])],
            [tok(BF16), ((GROUP, rows, rows), BF16)],
            f"query_attn_{g}",
        )

    def numer_state(g):
        numer[g] = call(
            functools.partial(numer_kernel, order_of(g)),
            [whole(first[g]), whole(second[g]), whole(feat_q[g]), whole(attn[g]), cols(value, g), cols(grad, g), cols(gain, g)],
            [sq(F32), tok(BF16), tok(BF16), sq(BF16), sq(BF16), ((GROUP, 8, HEAD), F32)],
            f"numer_{g}",
        )
        first_back[g] = hop_one(numer[g][0], g, 1)

    def later_hop(g):
        second_back[g] = hop_two(numer[g][0], first_back[g], g, 1)

    def query_grad(g):
        _, low, rest, ph, pl_, gains = numer[g]
        mixed[g], back_q[g], sum_q[g] = call(
            query_grad_kernel,
            [whole(x) for x in (low, rest, ph, pl_, feat_k[g])]
            + [cols(query, g), cols(value, g), wrows(w_query, g), whole(gains)],
            [((GROUP, rows, rows), BF16), tok(BF16), ((GROUP, HEAD + 8, HEAD), F32)],
            f"query_grad_{g}",
        )

    bases = {}

    def key_base(g):
        inputs = [whole(mixed[g]), whole(feat_q[g]), cols(key, g), wrows(w_key, g)]
        bases[g] = call(key_base_kernel, inputs, [tok(F32), tok(F32)], f"key_base_{g}")

    def key_grad(g):
        pre_k[g], late_h[g], late_l[g], sum_k[g] = call(
            functools.partial(key_grad_kernel, order_of(g)),
            [whole(first_back[g]), whole(second_back[g]), whole(bases[g][0]), whole(bases[g][1])]
            + [cols(key, g), cols(value, g)],
            [tok(BF16), sq(BF16), sq(BF16), sq(F32)],
            f"key_grad_{g}",
        )

    def value_grad(g):
        back_k[g], back_v[g] = call(
            value_grad_kernel,
            [whole(x) for x in (attn[g], numer[g][1], feat_k[g], late_h[g], late_l[g], pre_k[g])] + [wrows(w_key, g)],
            [tok(BF16), tok(BF16)],
            f"value_grad_{g}",
        )

    hops = {}

    def core_hop(b):
        parts = sum_q if b > 1 else sum_k
        inputs = [whole(parts[2 * (b % 2)]), whole(parts[2 * (b % 2) + 1])]
        shape = (2,) + parts[0].shape[1:]
        both = ((2,) + shape, F32)
        if b == 2:
            kept, sent = call(core_kernel, inputs, [both, both], "core_2")
            hops[b] = (kept, swap(sent, "dp", 1))
        elif b == 3:
            kept, sent, total = call(core_kernel, inputs + [whole(x) for x in hops[2]], [both] * 3, "core_3")
            hops[2] = (total, kept, swap(sent, "dp", 1))
        else:
            kept, *sent = call(core_kernel, inputs, [both, (shape, F32), (shape, F32)], f"core_{b}")
            hops[b] = (kept,) + tuple(swap(x, "dp", 1) for x in sent)

    def far_hop(_):
        kept, sent = call(far_kernel, [whole(x) for x in hops[2]], [(hops[2][0].shape, F32)] * 2, "far")
        hops[2] = (kept, swap(sent, "dp", 4))

    def near_hop(_):
        shape = hops[2][0].shape[1:]
        outs = [(shape, F32), (shape[1:], F32), (shape[1:], F32)]
        kept, *sent = call(near_kernel, [whole(x) for x in hops[2]], outs, "near")
        hops[2] = (kept,) + tuple(swap(x, "dp", 2) for x in sent)

    def z_hop(b):
        inputs = hops[0] + hops[1]
        own, *sent = call(spread_kernel, [whole(x) for x in inputs], [(inputs[1].shape, F32)] * 4, "spread")
        hops[0] = (own,) + tuple(swap(x, "dp", 2 * bits) for bits, x in enumerate(sent, 1))

    totals = {}

    def square(part):
        return (part,) + tuple(swap(part, "seq", bits) for bits in (1, 2, 3))

    def query_first(b):
        own, other = hops[2][0], hops[2][1 + b]
        (part,) = call(functools.partial(half_kernel, b), [whole(own), whole(other)], [(other.shape, F32)], f"query_sum_{b}")
        totals["query", b] = (part, swap(part, "seq", 1 + b))

    def query_second(b):
        part = pair(*totals["query", b], f"query_turn_{b}")
        totals["query", b] = (part, swap(part, "seq", 2 - b))

    def key_square(_):
        (part,) = call(gather_kernel, [whole(x) for x in hops[0]], [(hops[0][0].shape, F32)], "key_sum")
        totals["key"] = square(part)

    rows_out = ((2 * HEAD, HEAD), F32)

    def key_total(_):
        (totals["k"],) = call(key_total_kernel, [whole(x) for x in totals["key"]], [rows_out], "key_total")

    def query_total(_):
        totals["q"], totals["gain"] = call(
            query_total_kernel, [whole(x) for x in totals["query", 0] + totals["query", 1]], [rows_out, ((2, HEAD), F32)], "query_total"
        )

    def listed(by_group):
        return [by_group[g] for g in range(groups)]

    laid = {}

    def lay(k):
        parts = (back_q, back_k, back_v)[k]
        (laid[k],) = call(
            functools.partial(lay_kernel, groups),
            [whole(x) for x in listed(parts)],
            [((rows, width), BF16)],
            f"lay_{k}",
            [pltpu.VMEM((rows, width), BF16), pltpu.SemaphoreType.DMA(())],
            True,
        )

    if tuned:
        steps = (
            "K0K2Q0Q1p1p0Q2Q3p3p2N0N1G0G1N2N3a2G2G3",
            "l0l1a3l2l3B2P0P1H0H1a0V0V1P2P3H2H3a1V2V3Z0c2L0L1E0E1C0F0F1L2T0U0",
        )
        steps = "".join(steps)
    else:
        steps = "".join(f"K{g}" for g in range(0, groups, 2))
        steps += "".join(f"{kind}{g}" for kind in "pQNlGPHV" for g in range(groups)) + "L0L1L2"
    does = {
        "K": key_state,
        "p": prior_hop,
        "Q": query_attn,
        "N": numer_state,
        "l": later_hop,
        "G": query_grad,
        "P": key_base,
        "H": key_grad,
        "V": value_grad,
        "L": lay,
        "a": core_hop,
        "B": far_hop,
        "c": near_hop,
        "Z": z_hop,
        "E": query_first,
        "F": query_second,
        "C": key_square,
        "T": key_total,
        "U": query_total,
    }
    for k in range(0, len(steps), 2):
        does[steps[k]](int(steps[k + 1]))
    if tuned:
        total_q, total_k, total_gain = totals["q"], totals["k"], totals["gain"].reshape(2 * HEAD)
    else:

        def in_order(parts):
            return jnp.concatenate(listed(parts), axis=0)

        both = in_order(sum_q)
        owned = (
            lax.psum_scatter(both[:, :HEAD].reshape(width, HEAD), "dp", scatter_dimension=0, tiled=True),
            lax.psum_scatter(in_order(sum_k).reshape(width, HEAD), "dp", scatter_dimension=0, tiled=True),
            lax.psum_scatter(both[:, HEAD].reshape(width), "dp", scatter_dimension=0, tiled=True),
        )
        total_q, total_k, total_gain = lax.psum(owned, "seq")
    shape = query_in.shape
    return (
        laid[0].reshape(shape),
        laid[1].reshape(shape),
        laid[2].reshape(shape),
        total_q,
        total_k,
        total_gain,
    )


def solution(mesh):
    split = P("dp", "seq", None)
    return jax.shard_map(
        per_device,
        mesh=mesh,
        in_specs=(split, split, split, split, P(), P(), P()),
        out_specs=(split, split, split, P("dp", None), P("dp", None), P("dp")),
        check_vma=False,
    )
```

```python
import functools

import jax
import jax.numpy as jnp
from jax import lax
from jax.experimental import pallas as pl
from jax.experimental.pallas import tpu as pltpu
from jax.sharding import PartitionSpec as P

HEAD = 128
GROUP = 4
KEY_VMEM = (64 * 1024 - 4000, 64 * 1024 - 10000)
NORM_EPS = 1e-05
F32 = jnp.float32
BF16 = jnp.bfloat16


def dot(a, b, ca=1, cb=0):
    return lax.dot_general(a, b, (((ca,), (cb,)), ((), ())), preferred_element_type=F32)


def feature(pre):
    return jnp.where(pre > 0.0, pre + 1.0, jnp.exp(jnp.minimum(pre, 0.0)))


def split_low(value):
    high = value.astype(BF16)
    return high, (value - high.astype(F32)).astype(BF16)


def tril(rows):
    return lax.broadcasted_iota(jnp.int32, (rows, rows), 0) >= lax.broadcasted_iota(
        jnp.int32, (rows, rows), 1
    )


def columns(i):
    return slice(i * HEAD, (i + 1) * HEAD)


def place_in_square():
    mine = lax.axis_index("seq")
    return lax.rem(mine, 2), lax.div(mine, 2)


def summed(order, later, first, second):
    if order == "all":
        return [first[i] for i in range(GROUP)]
    at_x, at_y = place_in_square()
    if order == "xy":
        keep_first, keep_second = at_x != later, at_y != later
        return [
            jnp.where(keep_first, first[i], 0.0) + jnp.where(keep_second, second[i], 0.0) for i in range(GROUP)
        ]
    keep_first = at_y != later
    return [jnp.where(keep_first, first[i], 0.0) + second[i] for i in range(GROUP)]


def turn_kernel(later, own, first, out):
    at_x, at_y = place_in_square()
    out[...] = jnp.where(at_y != later, first[...], 0.0) + jnp.where(at_x == later, own[...], 0.0)


def bit_clear(bit):
    return lax.rem(lax.div(lax.axis_index("dp"), bit), 2) == 0


def key_features(key, w_key):
    return [feature(dot(key[:, c], w_key[c, :])).astype(BF16) for c in map(columns, range(2 * GROUP))]


def key_states(low, value, *outs):
    states = [dot(f, value[:, columns(i)], 0, 0) for i, f in enumerate(low)]
    for g in range(2):
        for i in range(GROUP):
            outs[2 * g][i] = low[g * GROUP + i]
            outs[2 * g + 1][i] = states[g * GROUP + i]


def key_kernel(block, key, value, w_key, *refs):
    outs, (key_buf, value_buf, w_buf, sems) = refs[:4], refs[4:]
    span = pl.ds(block * key_buf.shape[1], key_buf.shape[1])
    copies = [
        pltpu.make_async_copy(key.at[:, span], key_buf, sems.at[0]),
        pltpu.make_async_copy(w_key.at[span, :], w_buf, sems.at[1]),
        pltpu.make_async_copy(value.at[:, span], value_buf, sems.at[2]),
    ]
    for copy in copies:
        copy.start()
    copies[0].wait()
    copies[1].wait()
    low = key_features(key_buf, w_buf)
    copies[2].wait()
    key_states(low, value_buf, *outs)


def query_kernel(query, w_query, feat_key, feat_query, attn):
    causal = tril(query.shape[0])
    at = [columns(i) for i in range(GROUP)]
    low = [feature(dot(query[:, c], w_query[c, :])).astype(BF16) for c in at]
    scores = [dot(low[i], feat_key[i], 1, 1) for i in range(GROUP)]
    for i in range(GROUP):
        feat_query[i] = low[i]
        attn[i] = jnp.where(causal, scores[i], 0.0).astype(BF16)


def numer_kernel(order, first, second, feat_query, attn, value, grad, gain, adjoint, low_out, rest_out, ph_out, pl_out, gain_out):
    every = range(GROUP)
    at = [columns(i) for i in every]
    inner = [dot(attn[i], value[:, at[i]]) for i in every]
    prior = summed(order, 0, first, second)
    parts = [split_low(p) for p in prior]
    feat = [feat_query[i] for i in every]
    numer = [inner[i] + dot(feat[i], parts[i][0]) + dot(feat[i], parts[i][1]) for i in every]
    inv = [lax.rsqrt(jnp.mean(n * n, axis=-1, keepdims=True) + NORM_EPS) for n in numer]
    normed = [n * r for n, r in zip(numer, inv)]
    grad_f = [grad[:, c].astype(F32) for c in at]
    scaled = [x * gain[:, c] for x, c in zip(grad_f, at)]
    means = [jnp.mean(x * n, axis=-1, keepdims=True) for x, n in zip(scaled, normed)]
    grads = [split_low(inv[i] * (scaled[i] - normed[i] * means[i])) for i in every]
    states = [dot(feat[i], grads[i][0], 0, 0) for i in every]
    for i in every:
        adjoint[i] = states[i]
        low_out[i], rest_out[i] = grads[i]
        ph_out[i], pl_out[i] = parts[i]
        gain_out[i] = jnp.broadcast_to(jnp.sum(normed[i] * grad_f[i], axis=0, keepdims=True), (8, HEAD))


def query_grad_kernel(numer_low, rest, high, low, feat_key, query, value, w_query, gain, mixed_out, grad_out, weight):
    causal = tril(query.shape[0])
    every = range(GROUP)
    at = [columns(i) for i in every]
    grad_low = [numer_low[i] for i in every]
    slope = [jnp.minimum(feature(dot(query[:, c], w_query[c, :])), 1.0) for c in at]
    raw = [dot(grad_low[i], value[:, at[i]], 1, 1) for i in every]
    mixed = [jnp.where(causal, x, 0.0).astype(BF16) for x in raw]
    grad_fq = [
        dot(mixed[i], feat_key[i])
        + dot(grad_low[i], high[i], 1, 1)
        + dot(grad_low[i], low[i], 1, 1)
        + dot(rest[i], high[i], 1, 1)
        for i in every
    ]
    pre = [(grad_fq[i] * slope[i]).astype(BF16) for i in every]
    sums = [dot(query[:, at[i]], pre[i], 0, 0) for i in every]
    back = [dot(pre[i], w_query[at[i], :], 1, 1) for i in every]
    for i in every:
        mixed_out[i] = mixed[i]
        grad_out[i] = back[i].astype(BF16)
        weight[i, :HEAD, :] = sums[i]
        weight[i, HEAD:, :] = gain[i]


def key_base_kernel(mixed, feat_query, key, w_key, base_out, slope_out):
    every = range(GROUP)
    at = [columns(i) for i in every]
    slope = [jnp.minimum(feature(dot(key[:, c], w_key[c, :])), 1.0) for c in at]
    base = [dot(mixed[i], feat_query[i], 0, 0) for i in every]
    for i in every:
        base_out[i] = base[i]
        slope_out[i] = slope[i]


def key_grad_kernel(order, first, second, base, slope, key, value, pre_out, lh_out, ll_out, weight):
    every = range(GROUP)
    at = [columns(i) for i in every]
    parts = [split_low(x) for x in summed(order, 1, first, second)]
    val = [value[:, c] for c in at]
    grad_fk = [base[i] + dot(val[i], parts[i][0], 1, 1) + dot(val[i], parts[i][1], 1, 1) for i in every]
    pre = [(grad_fk[i] * slope[i]).astype(BF16) for i in every]
    sums = [dot(key[:, at[i]], pre[i], 0, 0) for i in every]
    for i in every:
        weight[i] = sums[i]
        pre_out[i] = pre[i]
        lh_out[i], ll_out[i] = parts[i]


def value_grad_kernel(attn, numer_low, feat_key, high, low, pre, w_key, key_out, value_out):
    every = range(GROUP)
    feat = [feat_key[i] for i in every]
    grads = [
        dot(attn[i], numer_low[i], 0, 0) + dot(feat[i], high[i]) + dot(feat[i], low[i]) for i in every
    ]
    back = [dot(pre[i], w_key[columns(i), :], 1, 1) for i in every]
    for i in every:
        value_out[i] = grads[i].astype(BF16)
        key_out[i] = back[i].astype(BF16)


def lay_kernel(groups, *refs):
    out, laid, sem = refs[groups:]
    for g in range(groups):
        for i in range(GROUP):
            laid[:, place(g, i)] = refs[g][i]
    copy = pltpu.make_async_copy(laid, out, sem)
    copy.start()
    copy.wait()


def pair_kernel(one, two, out):
    out[...] = one[...] + two[...]


def core_kernel(low, high, *refs):
    if len(refs) == 5:
        one, two, kept, *sent, total = refs
        total[...] = one[...] + two[...]
    else:
        kept, *sent = refs
    first = bit_clear(1)
    for m, part in enumerate((low, high)):
        for b in range(2):
            one, two = part[b], part[2 + b]
            kept[m, b] = jnp.where(first, one, two)
            out = jnp.where(first, two, one)
            if len(sent) == 2:
                sent[m][b] = out
            else:
                sent[0][m, b] = out


def far_kernel(low, own, theirs, kept, sent):
    first = bit_clear(4)
    high = own[...] + theirs[...]
    kept[...] = jnp.where(first, low[...], high)
    sent[...] = jnp.where(first, high, low[...])


def near_kernel(mine, theirs, kept, *sent):
    first = bit_clear(2)
    one, two = mine[0] + theirs[0], mine[1] + theirs[1]
    kept[...] = jnp.where(first, one, two)
    out = jnp.where(first, two, one)
    for b in range(2):
        sent[b][...] = out[b]


def spread_kernel(*refs):
    parts, outs = refs[:6], refs[6:]
    near, far = bit_clear(2), bit_clear(4)
    for m in range(2):
        low = parts[0][m] + parts[1 + m][...]
        high = parts[3][m] + parts[4 + m][...]
        here, there = jnp.where(far, low, high), jnp.where(far, high, low)
        same = near if m == 0 else jnp.logical_not(near)

        @pl.when(same)
        def _():
            outs[0][...] = here
            outs[2][...] = there

        @pl.when(jnp.logical_not(same))
        def _():
            outs[1][...] = here
            outs[3][...] = there


def gather_kernel(own, near, far, both, out):
    out[...] = (own[...] + near[...]) + (far[...] + both[...])


def half_kernel(b, own, other, out):
    out[...] = own[b] + other[...]


def key_total_kernel(key, key_x, key_y, key_d, out):
    total = (key[...] + key_x[...]) + (key_y[...] + key_d[...])
    for b in range(2):
        out[b * HEAD : (b + 1) * HEAD, :] = total[b]


def query_total_kernel(even, even_other, odd, odd_other, out, out_gain):
    for b, (one, two) in enumerate(((even, even_other), (odd, odd_other))):
        total = one[...] + two[...]
        out[b * HEAD : (b + 1) * HEAD, :] = total[:HEAD, :]
        out_gain[b : b + 1, :] = total[HEAD : HEAD + 1, :]


def place(g, i):
    at = (g * GROUP + i) * HEAD
    return slice(at, at + HEAD)


class Order:
    def __init__(self):
        self.last = None

    def __call__(self, body, ins, outs, name, scratch=(), to_hbm=False, to_vmem=False, chain=True, vmem=12 * 1024):
        at = len(ins)
        after = chain and self.last is not None
        if after:
            ins = ins + [(self.last, pl.BlockSpec(memory_space=pl.ANY))]
        inputs, results = len(ins), len(outs)

        def ordered(*refs):
            body(*refs[:at], *refs[inputs : inputs + results], *refs[inputs + results + chain :])
            if chain:
                token = refs[inputs + results]
                token[...] = jnp.zeros_like(token)

        out_specs = [
            pl.BlockSpec(memory_space=pltpu.HBM) if to_hbm else pl.BlockSpec(shape, lambda _, n=len(shape): (0,) * n)
            for shape, _ in outs
        ]
        out_shape = [jax.ShapeDtypeStruct(shape, kind) for shape, kind in outs]
        if to_vmem:
            out_specs = [pl.BlockSpec(memory_space=pltpu.VMEM) for _ in outs]
            out_shape = [pltpu.VMEM(shape, kind) for shape, kind in outs]
        if chain and to_vmem:
            out_specs.append(pl.BlockSpec(memory_space=pltpu.VMEM))
            out_shape.append(pltpu.VMEM((8, HEAD), F32))
        elif chain:
            out_specs.append(pl.BlockSpec((8, HEAD), lambda _: (0, 0)))
            out_shape.append(jax.ShapeDtypeStruct((8, HEAD), F32))
        result = pl.pallas_call(
            ordered,
            grid=(1,),
            in_specs=[spec for _, spec in ins],
            out_specs=out_specs,
            out_shape=out_shape,
            scratch_shapes=list(scratch),
            compiler_params=pltpu.CompilerParams(vmem_limit_bytes=vmem * 1024),
            cost_estimate=pl.CostEstimate(flops=200000000, bytes_accessed=0, transcendentals=0),
            name=name,
        )(*[x for x, _ in ins])
        if chain:
            self.last = result[-1]
            return result[:-1]
        return result


def whole(x):
    return (x, pl.BlockSpec(x.shape, lambda _, n=x.ndim: (0,) * n))


def in_hbm(x):
    return (x, pl.BlockSpec(memory_space=pltpu.HBM))


def scan_generic(value, reverse):
    peers, mine = lax.axis_size("seq"), lax.axis_index("seq")
    everything = lax.all_gather(value, "seq")

    def turn(k, before):
        reached = k > mine if reverse else k < mine
        return before + jnp.where(reached, everything[k], 0.0)

    return lax.fori_loop(0, peers, turn, jnp.zeros_like(value))


def swap(value, axis, bit):
    return lax.ppermute(value, axis, [(i, i ^ bit) for i in range(lax.axis_size(axis))])


def per_device(query_in, key_in, value_in, grad_out, w_query, w_key, norm_gain):
    _, rows, width = query_in.shape
    heads = width // HEAD
    groups = heads // GROUP
    tuned = lax.axis_size("seq") == 4 and lax.axis_size("dp") == 8 and heads == 16
    query, key, value, grad = (x.reshape(rows, width) for x in (query_in, key_in, value_in, grad_out))
    gain = norm_gain.reshape(1, width)
    wide = GROUP * HEAD

    def cols(x, g):
        return (x, pl.BlockSpec((x.shape[0], wide), lambda _: (0, g)))

    def wrows(x, g):
        return (x, pl.BlockSpec((wide, HEAD), lambda _: (g, 0)))

    def tok(kind):
        return ((GROUP, rows, HEAD), kind)

    def sq(kind):
        return ((GROUP, HEAD, HEAD), kind)

    call = Order()

    def pair(one, two, name):
        (out,) = call(pair_kernel, [whole(one), whole(two)], [(one.shape, F32)], name)
        return out

    feat_k, state, feat_q, attn = {}, {}, {}, {}
    numer, mixed, back_q, sum_q = {}, {}, {}, {}
    pre_k, late_h, late_l, sum_k, back_k, back_v = {}, {}, {}, {}, {}, {}
    first, second, first_back, second_back = {}, {}, {}, {}

    def order_of(g):
        if not tuned:
            return "all"
        return ("xy", "yx")[g % 2]

    def hop_one(value, g, later):
        if not tuned:
            return scan_generic(value, later == 1)
        return swap(value, "seq", 1 if order_of(g) == "xy" else 2)

    def hop_two(value, brought, g, later):
        if not tuned:
            return brought
        if order_of(g) == "xy":
            return swap(pair(value, brought, f"pair_{later}_{g}"), "seq", 2)
        body = functools.partial(turn_kernel, later)
        (out,) = call(body, [whole(value), whole(brought)], [(value.shape, F32)], f"turn_{later}_{g}")
        return swap(out, "seq", 1)

    def key_state(g):
        outs = [tok(BF16), sq(F32)] * 2
        pair_wide = 2 * wide
        scratch = [
            pltpu.VMEM((rows, pair_wide), BF16),
            pltpu.VMEM((rows, pair_wide), BF16),
            pltpu.VMEM((pair_wide, HEAD), BF16),
            pltpu.SemaphoreType.DMA((3,)),
        ]
        inputs = [in_hbm(key), in_hbm(value), in_hbm(w_key)]
        body = functools.partial(key_kernel, g // 2)
        result = call(body, inputs, outs, f"key_state_{g}", scratch, to_vmem=True, vmem=KEY_VMEM[min(g // 2, 1)])
        feat_k[g], state[g], feat_k[g + 1], state[g + 1] = result
        for k in (g, g + 1):
            first[k] = hop_one(state[k], k, 0)

    def prior_hop(g):
        second[g] = hop_two(state[g], first[g], g, 0)

    def query_attn(g):
        feat_q[g], attn[g] = call(
            query_kernel,
            [cols(query, g), wrows(w_query, g), whole(feat_k[g])],
            [tok(BF16), ((GROUP, rows, rows), BF16)],
            f"query_attn_{g}",
        )

    def numer_state(g):
        numer[g] = call(
            functools.partial(numer_kernel, order_of(g)),
            [whole(first[g]), whole(second[g]), whole(feat_q[g]), whole(attn[g]), cols(value, g), cols(grad, g), cols(gain, g)],
            [sq(F32), tok(BF16), tok(BF16), sq(BF16), sq(BF16), ((GROUP, 8, HEAD), F32)],
            f"numer_{g}",
        )
        first_back[g] = hop_one(numer[g][0], g, 1)

    def later_hop(g):
        second_back[g] = hop_two(numer[g][0], first_back[g], g, 1)

    def query_grad(g):
        _, low, rest, ph, pl_, gains = numer[g]
        mixed[g], back_q[g], sum_q[g] = call(
            query_grad_kernel,
            [whole(x) for x in (low, rest, ph, pl_, feat_k[g])]
            + [cols(query, g), cols(value, g), wrows(w_query, g), whole(gains)],
            [((GROUP, rows, rows), BF16), tok(BF16), ((GROUP, HEAD + 8, HEAD), F32)],
            f"query_grad_{g}",
        )

    bases = {}

    def key_base(g):
        inputs = [whole(mixed[g]), whole(feat_q[g]), cols(key, g), wrows(w_key, g)]
        bases[g] = call(key_base_kernel, inputs, [tok(F32), tok(F32)], f"key_base_{g}")

    def key_grad(g):
        pre_k[g], late_h[g], late_l[g], sum_k[g] = call(
            functools.partial(key_grad_kernel, order_of(g)),
            [whole(first_back[g]), whole(second_back[g]), whole(bases[g][0]), whole(bases[g][1])]
            + [cols(key, g), cols(value, g)],
            [tok(BF16), sq(BF16), sq(BF16), sq(F32)],
            f"key_grad_{g}",
        )

    def value_grad(g):
        back_k[g], back_v[g] = call(
            value_grad_kernel,
            [whole(x) for x in (attn[g], numer[g][1], feat_k[g], late_h[g], late_l[g], pre_k[g])] + [wrows(w_key, g)],
            [tok(BF16), tok(BF16)],
            f"value_grad_{g}",
        )

    hops = {}

    def core_hop(b):
        parts = sum_q if b > 1 else sum_k
        inputs = [whole(parts[2 * (b % 2)]), whole(parts[2 * (b % 2) + 1])]
        shape = (2,) + parts[0].shape[1:]
        both = ((2,) + shape, F32)
        if b == 2:
            kept, sent = call(core_kernel, inputs, [both, both], "core_2")
            hops[b] = (kept, swap(sent, "dp", 1))
        elif b == 3:
            kept, sent, total = call(core_kernel, inputs + [whole(x) for x in hops[2]], [both] * 3, "core_3")
            hops[2] = (total, kept, swap(sent, "dp", 1))
        else:
            kept, *sent = call(core_kernel, inputs, [both, (shape, F32), (shape, F32)], f"core_{b}")
            hops[b] = (kept,) + tuple(swap(x, "dp", 1) for x in sent)

    def far_hop(_):
        kept, sent = call(far_kernel, [whole(x) for x in hops[2]], [(hops[2][0].shape, F32)] * 2, "far")
        hops[2] = (kept, swap(sent, "dp", 4))

    def near_hop(_):
        shape = hops[2][0].shape[1:]
        outs = [(shape, F32), (shape[1:], F32), (shape[1:], F32)]
        kept, *sent = call(near_kernel, [whole(x) for x in hops[2]], outs, "near")
        hops[2] = (kept,) + tuple(swap(x, "dp", 2) for x in sent)

    def z_hop(b):
        inputs = hops[0] + hops[1]
        own, *sent = call(spread_kernel, [whole(x) for x in inputs], [(inputs[1].shape, F32)] * 4, "spread")
        hops[0] = (own,) + tuple(swap(x, "dp", 2 * bits) for bits, x in enumerate(sent, 1))

    totals = {}

    def square(part):
        return (part,) + tuple(swap(part, "seq", bits) for bits in (1, 2, 3))

    def query_first(b):
        own, other = hops[2][0], hops[2][1 + b]
        (part,) = call(functools.partial(half_kernel, b), [whole(own), whole(other)], [(other.shape, F32)], f"query_sum_{b}")
        totals["query", b] = (part, swap(part, "seq", 1 + b))

    def query_second(b):
        part = pair(*totals["query", b], f"query_turn_{b}")
        totals["query", b] = (part, swap(part, "seq", 2 - b))

    def key_square(_):
        (part,) = call(gather_kernel, [whole(x) for x in hops[0]], [(hops[0][0].shape, F32)], "key_sum")
        totals["key"] = square(part)

    rows_out = ((2 * HEAD, HEAD), F32)

    def key_total(_):
        (totals["k"],) = call(key_total_kernel, [whole(x) for x in totals["key"]], [rows_out], "key_total")

    def query_total(_):
        totals["q"], totals["gain"] = call(
            query_total_kernel, [whole(x) for x in totals["query", 0] + totals["query", 1]], [rows_out, ((2, HEAD), F32)], "query_total"
        )

    def listed(by_group):
        return [by_group[g] for g in range(groups)]

    laid = {}

    def lay(k):
        parts = (back_q, back_k, back_v)[k]
        (laid[k],) = call(
            functools.partial(lay_kernel, groups),
            [whole(x) for x in listed(parts)],
            [((rows, width), BF16)],
            f"lay_{k}",
            [pltpu.VMEM((rows, width), BF16), pltpu.SemaphoreType.DMA(())],
            True,
        )

    if tuned:
        steps = (
            "K0K2Q0Q1p1p0Q2Q3p3p2N0N1G0G1N2N3a2G2G3",
            "l0l1a3P0P1P2P3l2l3B2H0H1a0V0V1H2H3a1V2V3Z0c2L0L1E0E1C0F0F1L2T0U0",
        )
        steps = "".join(steps)
    else:
        steps = "".join(f"K{g}" for g in range(0, groups, 2))
        steps += "".join(f"{kind}{g}" for kind in "pQNlGPHV" for g in range(groups)) + "L0L1L2"
    does = {
        "K": key_state,
        "p": prior_hop,
        "Q": query_attn,
        "N": numer_state,
        "l": later_hop,
        "G": query_grad,
        "P": key_base,
        "H": key_grad,
        "V": value_grad,
        "L": lay,
        "a": core_hop,
        "B": far_hop,
        "c": near_hop,
        "Z": z_hop,
        "E": query_first,
        "F": query_second,
        "C": key_square,
        "T": key_total,
        "U": query_total,
    }
    for k in range(0, len(steps), 2):
        does[steps[k]](int(steps[k + 1]))
    if tuned:
        total_q, total_k, total_gain = totals["q"], totals["k"], totals["gain"].reshape(2 * HEAD)
    else:

        def in_order(parts):
            return jnp.concatenate(listed(parts), axis=0)

        both = in_order(sum_q)
        owned = (
            lax.psum_scatter(both[:, :HEAD].reshape(width, HEAD), "dp", scatter_dimension=0, tiled=True),
            lax.psum_scatter(in_order(sum_k).reshape(width, HEAD), "dp", scatter_dimension=0, tiled=True),
            lax.psum_scatter(both[:, HEAD].reshape(width), "dp", scatter_dimension=0, tiled=True),
        )
        total_q, total_k, total_gain = lax.psum(owned, "seq")
    shape = query_in.shape
    return (
        laid[0].reshape(shape),
        laid[1].reshape(shape),
        laid[2].reshape(shape),
        total_q,
        total_k,
        total_gain,
    )


def solution(mesh):
    split = P("dp", "seq", None)
    return jax.shard_map(
        per_device,
        mesh=mesh,
        in_specs=(split, split, split, split, P(), P(), P()),
        out_specs=(split, split, split, P("dp", None), P("dp", None), P("dp")),
        check_vma=False,
    )
```
